256 devices in a mesh: dp: 32 (over y, x, core), seq: 8 (over z).
Axes of the slice: x: 4, y: 4, z: 8, core: 2. Of those that a mesh axis runs over, the one named last changes fastest.
Arguments:
- features: bfloat16 [64, 24, 32, 1536], P('dp', 'seq'), may hold values from -6 to 6
- enc_gain: float32 [1536], replicated, may hold values from 0.25 to 4
- enc_bias: float32 [1536], replicated, may hold values from -0.02 to 0.02
- row_source: int32 [64, 48], P('dp', 'seq'), may hold values from 0 to 22, as said below
- timesteps: int32 [64], P('dp'), may hold values from 0 to 999
- pre_act: bfloat16 [64, 48, 64, 2048], P('dp', 'seq'), may hold values from -8 to 8
- proj_weight: bfloat16 [2048, 1536], P('dp'), may hold values from -0.125 to 0.125
- proj_bias: float32 [1536], replicated, may hold values from -3 to 3
Outputs:
- pre_grad: bfloat16 [64, 48, 64, 2048], P('dp', 'seq')
- weight_grad: float32 [2048, 1536], P('dp')
The draws below stay inside these ranges and needn't reach their ends.
Inputs may be any that keep to these rules, and one draw needn't show every extreme that they name: row_source[b, r] lies between r // 2 - 2 and r // 2 + 1.
All inputs are finite; a program needn't handle non-finite values.
Results may differ from the reference program's by a relative error of at most 0.0057.
Values may be sent and summed in bfloat16 or wider, within the bound.
No kernel may reach another device: no remote copies, remote signals or barrier semaphores. Data moves between devices by JAX's collectives and lax.ppermute only.
A program may use at most 128 MiB of HBM per device.

```python
import math
import jax
import jax.numpy as jnp
from jax import lax

DE = 1536
PH = 2048
EC = 32
ER = 24
TR = 48
TC = 64
IMAGES = 64


def draw_row_source(key, part):
    key = jax.random.fold_in(key, 11)
    jitter = jax.random.randint(key, (IMAGES, 1), -1, 2)
    target = jnp.arange(TR, dtype=jnp.int32)[None, :]
    low_row = jnp.where(target % 2 == 1, (target - 1) // 2, target // 2 - 1)
    return jnp.clip(low_row + jitter, 0, ER - 2).astype(jnp.int32)


def set_ends(array, rng, least, largest):
    shape = array.shape
    place = [jax.random.randint(jax.random.fold_in(rng, axis), (), 0, shape[axis]) for axis in range(len(shape))]
    array = array.at[tuple(place)].set(least)
    longest = shape.index(max(shape))
    place[longest] = (place[longest] + 1) % shape[longest]
    return array.at[tuple(place)].set(largest)


def raised(result, stream_key, source, target, parts, factor):
    owner, partner = [(jnp.arange(result.shape[dim]) // (result.shape[dim] // parts)).reshape([-1 if axis == dim else 1 for axis in range(result.ndim)]) for dim in (source, target)]
    chosen = jax.random.permutation(stream_key, parts)[partner]
    strong = (owner == chosen) | (owner == (partner + parts // 2) % parts)
    return jnp.where(strong, factor * result, result)


def shard_levels(key, extent, cuts, least, high):
    def one(axis_at, blocks):
        draws = jax.random.uniform(jax.random.fold_in(jax.random.fold_in(key, 6), axis_at), (blocks,), jnp.float32, least / len(cuts), high / len(cuts))
        return jnp.repeat(jnp.exp(draws), extent[axis_at] // blocks).reshape((-1,) + (1,) * (len(extent) - axis_at - 1))

    factor_of = one(*cuts[0])
    for cut in cuts[1:]:
        factor_of = factor_of * one(*cut)
    return factor_of


def bell_draw(rng, extent, scale, most, split=(), kind=jnp.bfloat16):
    array = scale * jax.random.normal(rng, extent, jnp.float32)
    if split:
        array = array * shard_levels(rng, extent, split, -0.22, 0.18)
    return jnp.clip(array, -most, most).astype(kind)


def heavy_noise(own_key, shape, width, reach, pieces, heavy, kind=jnp.bfloat16):
    drawn = width * jax.random.normal(own_key, shape, jnp.float32)
    if pieces:
        drawn = drawn * shard_levels(own_key, shape, pieces, -0.22, 0.18)
    return jnp.clip(raised(drawn, jax.random.fold_in(own_key, 3), *heavy), -reach, reach).astype(kind)


def setup_inputs(seed: int = 0) -> dict:
    keys = jax.random.split(jax.random.key(seed), 9)
    features = bell_draw(keys[0], (IMAGES, ER, EC, DE), 1.0, 6.0, ((0, 32), (1, 8)))
    enc_gain = jnp.clip(jnp.exp(jax.random.uniform(keys[1], (DE,), jnp.float32, math.log(0.25), math.log(4.0))), 0.25, 4.0)
    enc_bias = jnp.clip(jax.random.uniform(keys[2], (DE,), jnp.float32, -0.02, 0.02), -0.02, 0.02)
    row_source = draw_row_source(jax.random.fold_in(keys[8], 71), 0)
    timesteps = set_ends(jax.random.randint(keys[4], (IMAGES,), 0, 1000), jax.random.fold_in(keys[4], 1), 0, 999).astype(jnp.int32)
    pre_act = heavy_noise(keys[5], (IMAGES, TR, TC, PH), 1.5, 8.0, ((0, 32), (1, 8)), (0, 3, 32, 2.75))
    proj_weight = bell_draw(keys[6], (PH, DE), PH ** -0.5, 0.125, ((0, 32),))
    proj_bias = bell_draw(keys[7], (DE,), 0.5, 3.0, (), jnp.float32)
    return {"features": features, "enc_gain": enc_gain, "enc_bias": enc_bias, "row_source": row_source, "timesteps": timesteps, "pre_act": pre_act, "proj_weight": proj_weight, "proj_bias": proj_bias}


loss_scale = 1024.0
norm_eps = 1e-06
highest = lax.Precision.HIGHEST

def layer_norm(values_in, gain_vec, bias_vec):
    values = values_in.astype(jnp.float32)
    center = values - lax.optimization_barrier(jnp.mean(values, axis=-1, keepdims=True))
    spread = lax.optimization_barrier(jnp.mean(center * center, axis=-1, keepdims=True))
    return (center * lax.rsqrt(spread + norm_eps) * gain_vec + bias_vec).astype(jnp.bfloat16)

def blend_matrix(low_row, weight_high, source_len):
    column = jnp.arange(source_len, dtype=jnp.int32)[None, :]
    low_idx = jnp.clip(low_row, 0, source_len - 1)[:, None]
    high_idx = jnp.clip(low_row + 1, 0, source_len - 1)[:, None]
    return (1.0 - weight_high)[:, None] * (column == low_idx).astype(jnp.float32) + weight_high[:, None] * (column == high_idx).astype(jnp.float32)

def parity_weight(target):
    return jnp.where(target % 2 == 1, 0.25, 0.75).astype(jnp.float32)

def column_blend(source_len):
    target = jnp.arange(2 * source_len, dtype=jnp.int32)
    low_row = jnp.where(target % 2 == 1, (target - 1) // 2, target // 2 - 1)
    return blend_matrix(low_row, parity_weight(target), source_len)

def cosine_grad(projected, target, image_weight):
    proj_norm = jnp.sqrt(lax.optimization_barrier(jnp.sum(projected * projected, axis=-1, keepdims=True)) + norm_eps)
    target_norm = jnp.sqrt(lax.optimization_barrier(jnp.sum(target * target, axis=-1, keepdims=True)) + norm_eps)
    cosine = lax.optimization_barrier(jnp.sum(projected * target, axis=-1, keepdims=True)) / (proj_norm * target_norm)
    scaled = -loss_scale * image_weight
    return (scaled * (target / (proj_norm * target_norm) - cosine * projected / (proj_norm * proj_norm))).astype(jnp.bfloat16)

def silu_slope(pre_vals):
    sigma = jax.nn.sigmoid(pre_vals)
    return sigma * (1.0 + pre_vals * (1.0 - sigma))

def reference(features, enc_gain, enc_bias, row_source, timesteps, pre_act, proj_weight, proj_bias):
    col_matrix = column_blend(EC)
    parity = parity_weight(jnp.arange(TR, dtype=jnp.int32))

    def one_image(carry, inputs):
        feats_img, rows_img, step_img, pre_img = inputs
        normed = layer_norm(feats_img, enc_gain, enc_bias)
        row_matrix = blend_matrix(rows_img.astype(jnp.int32), parity, ER)
        blended = jnp.einsum('cj,kje->kce', col_matrix, normed.astype(jnp.float32), precision=highest)
        target = jnp.einsum('rk,kce->rce', row_matrix, blended, precision=highest)
        target = target.reshape(TR * TC, DE)
        hidden_in = pre_img.reshape(TR * TC, PH).astype(jnp.float32)
        active = jax.nn.silu(hidden_in).astype(jnp.bfloat16)
        projected = jnp.dot(active, proj_weight, preferred_element_type=jnp.float32) + proj_bias
        image_weight = 1.0 - step_img.astype(jnp.float32) / 1000.0
        out_grad = cosine_grad(projected, target, image_weight)
        active_grad = jnp.dot(out_grad, proj_weight.T, preferred_element_type=jnp.float32)
        pre_grad = (active_grad * silu_slope(hidden_in)).astype(jnp.bfloat16).reshape(TR, TC, PH)
        carry = carry + jnp.dot(active.T, out_grad, preferred_element_type=jnp.float32)
        return (carry, pre_grad)
    weight_grad, pre_grad = lax.scan(one_image, jnp.zeros((PH, DE), jnp.float32), (features, row_source, timesteps, pre_act))
    return (pre_grad, weight_grad)
```

```python
import functools

import jax
import jax.numpy as jnp
from jax import lax
from jax.experimental import pallas as pl
from jax.experimental.pallas import tpu as pltpu
from jax.sharding import Mesh, PartitionSpec as P

loss_scale = 1024.0
norm_eps = 1e-06
MIB = 1 << 20
bf16, f32 = jnp.bfloat16, jnp.float32
VMEM = pltpu.VMEM
SMEM = pltpu.SMEM


def shift(block, axis, step):
    count = lax.axis_size(axis)
    return lax.ppermute(block, axis, [(i, (i + step) % count) for i in range(count)])


def params(mib, steps=0):
    semantics = ("arbitrary",) * steps if steps else None
    return pltpu.CompilerParams(vmem_limit_bytes=mib * MIB, dimension_semantics=semantics)


def cost(flops, nbytes, trans=0):
    return pl.CostEstimate(flops=flops, bytes_accessed=nbytes, transcendentals=trans)


def gather_ring(top, bottom, axis):
    left_top = shift(top, axis, 1)
    right_bottom = shift(bottom, axis, -1)
    left_bottom = shift(bottom, axis, 1)
    right_top = shift(top, axis, -1)
    far_top = shift(left_top, axis, 1)
    far_bottom = shift(right_bottom, axis, -1)
    return [(top, bottom), (right_top, right_bottom), (far_top, far_bottom), (left_top, left_bottom)]


def scatter_ring(blocks, axis):
    far_top = shift(blocks[2][0].astype(bf16), axis, 1)
    far_bottom = shift(blocks[2][1].astype(bf16), axis, -1)
    from_left_bottom = shift(blocks[1][1].astype(bf16), axis, 1)
    from_right_top = shift(blocks[3][0].astype(bf16), axis, -1)
    from_left_top = shift((blocks[1][0].astype(f32) + far_top.astype(f32)).astype(bf16), axis, 1)
    from_right_bottom = shift((blocks[3][1].astype(f32) + far_bottom.astype(f32)).astype(bf16), axis, -1)
    top = blocks[0][0].astype(f32) + from_right_top.astype(f32) + from_left_top.astype(f32)
    bottom = blocks[0][1].astype(f32) + from_left_bottom.astype(f32) + from_right_bottom.astype(f32)
    return top, bottom


def gather_weight(weight):
    first_a = gather_ring(weight[0:16], weight[16:32], "y")
    first_b = gather_ring(weight[32:48], weight[48:64], "x")
    halves = []
    for first, axis in ((first_a, "x"), (first_b, "y")):
        top = jnp.concatenate([first[0][0], first[0][1], first[1][0], first[1][1]], axis=0)
        bottom = jnp.concatenate([first[2][0], first[2][1], first[3][0], first[3][1]], axis=0)
        halves.append(gather_ring(top, bottom, axis))
    return halves


def silu_kernel(place_ref, pre_ref, out_ref):
    step = pl.program_id(0)
    my_y, my_x, my_c = place_ref[0], place_ref[1], place_ref[2]
    dy = (step // 4 - my_y + 4) % 4
    dx = (step % 4 - my_x + 4) % 4
    p = pre_ref[...].astype(f32)
    active = (p * jax.nn.sigmoid(p)).astype(bf16)
    turned = active.T
    for c in range(2):
        dc = (c - my_c + 2) % 2
        for kind in range(2):
            spot = dx * 4 + dy if kind == 0 else dy * 4 + dx
            row = pl.multiple_of(dc * 1024 + kind * 512 + spot * 32, 32)
            out_ref[pl.ds(row, 32), :] = turned[c * 64 + kind * 32 : c * 64 + kind * 32 + 32, :]


def hidden_rows(place, pre):
    tokens, hidden = pre.shape
    return pl.pallas_call(
        silu_kernel,
        grid=(hidden // 128,),
        in_specs=[
            pl.BlockSpec(memory_space=SMEM),
            pl.BlockSpec((tokens, 128), lambda i: (0, i)),
        ],
        out_specs=pl.BlockSpec((hidden, tokens), lambda i: (0, 0)),
        out_shape=jax.ShapeDtypeStruct((hidden, tokens), bf16),
        compiler_params=params(16, 1),
        cost_estimate=cost(tokens * hidden * 8, tokens * hidden * 4, tokens * hidden),
        name="hidden_rows",
    )(place, pre)


def target_kernel(low_ref, left_ref, mid_ref, right_ref, gain_ref, bias_ref, out_ref, sum_ref, ext_ref):
    gain, bias = gain_ref[...], bias_ref[...]
    width = gain.shape[-1]
    for b in range(2):
        row = 0
        for ref, count in ((left_ref, 2), (mid_ref, 3), (right_ref, 2)):
            for k in range(count):
                x = ref[b, k].astype(f32)
                center = x - jnp.sum(x, axis=-1, keepdims=True) * (1.0 / width)
                spread = jnp.sum(center * center, axis=-1, keepdims=True) * (1.0 / width)
                ext_ref[b, row : row + 32, :] = (center * lax.rsqrt(spread + norm_eps) * gain + bias).astype(bf16)
                row += 32
    c = lax.broadcasted_iota(jnp.int32, (64, 224), 0)
    lane = lax.broadcasted_iota(jnp.int32, (64, 224), 1)
    source, j = lane // 32, lane % 32
    odd = c % 2 == 1
    low = jnp.where(odd, (c - 1) // 2, c // 2 - 1)
    high_w = jnp.where(odd, 0.25, 0.75).astype(f32)
    columns = jnp.where(j == jnp.clip(low, 0, 31), 1.0 - high_w, 0.0) + jnp.where(
        j == jnp.clip(low + 1, 0, 31), high_w, 0.0
    )
    for b in range(2):
        for r in range(6):
            h = 0.25 if r % 2 == 1 else 0.75
            first = low_ref[b, r]
            rows = jnp.where(source == first, 1.0 - h, 0.0) + jnp.where(source == first + 1, h, 0.0)
            blend = (columns * rows).astype(bf16)
            target = jnp.dot(blend, ext_ref[b], preferred_element_type=f32)
            at = (b * 6 + r) * 64
            out_ref[at : at + 64, :] = target
            sum_ref[at : at + 64, :] = jnp.broadcast_to(jnp.sum(target * target, axis=-1, keepdims=True), (64, 128))


def make_target(local_low, left, mid, right, gain, bias):
    width = gain.shape[-1]
    whole = pl.BlockSpec(memory_space=VMEM)
    return pl.pallas_call(
        target_kernel,
        in_specs=[pl.BlockSpec(memory_space=SMEM)] + [whole] * 5,
        out_specs=[whole, whole],
        out_shape=[jax.ShapeDtypeStruct((768, width), f32), jax.ShapeDtypeStruct((768, 128), f32)],
        scratch_shapes=[pltpu.VMEM((2, 224, width), bf16)],
        compiler_params=params(24),
        cost_estimate=cost(2 * 768 * 224 * width, 768 * width * 8),
        name="make_target",
    )(local_low, left, mid, right, gain.reshape(1, -1), bias.reshape(1, -1))


def place_piece(w_ref, piece_ref, place_ref, dc, kind, offset, half):
    my_y, my_x, my_c = place_ref[0], place_ref[1], place_ref[2]
    core = (my_c + dc) % 2
    for q in range(2):
        inner = half * 2 + q
        dx, dy = (offset, inner) if kind == 0 else (inner, offset)
        block = ((my_y + dy) % 4) * 4 + (my_x + dx) % 4
        row = pl.multiple_of(block * 128 + core * 64 + kind * 32, 32)
        w_ref[pl.ds(row, 32), :] = piece_ref[q * 32 : q * 32 + 32, :]


def grad_kernel(keys, place_ref, scale_ref, act_ref, target_ref, tsum_ref, pbias_ref, *refs):
    pieces, (w_ref, out_ref, proj_ref, pp_ref, pt_ref) = refs[: len(keys)], refs[len(keys) :]
    for (dc, kind, offset, half), piece_ref in zip(keys, pieces):
        place_piece(w_ref, piece_ref, place_ref, dc, kind, offset, half)
    width = out_ref.shape[1]
    step = 256
    pp_ref[...] = jnp.zeros_like(pp_ref)
    pt_ref[...] = jnp.zeros_like(pt_ref)

    @pl.loop(0, width // step)
    def _(n):
        at = pl.ds(pl.multiple_of(n * step, step), step)
        proj = jnp.dot(act_ref[...], w_ref[:, at], preferred_element_type=f32) + pbias_ref[:, at]
        proj_ref[:, at] = proj
        target = target_ref[:, at]
        square, cross = proj * proj, proj * target
        pp_ref[...] += square[:, :128] + square[:, 128:]
        pt_ref[...] += cross[:, :128] + cross[:, 128:]

    half_tokens = out_ref.shape[0] // 2
    for part in range(12):
        rows = slice(part * 64, part * 64 + 64)
        scaled = -loss_scale * scale_ref[part * 64 // half_tokens]
        pn2 = jnp.sum(pp_ref[rows, :], axis=-1, keepdims=True) + norm_eps
        pt = jnp.sum(pt_ref[rows, :], axis=-1, keepdims=True)
        tn2 = tsum_ref[rows, 0:1] + norm_eps
        inv = lax.rsqrt(pn2) * lax.rsqrt(tn2)
        near = scaled * inv
        along = scaled * (pt * inv) / pn2
        out_ref[rows, :] = (near * target_ref[rows, :] - along * proj_ref[rows, :]).astype(bf16)


def weight_and_grad(place, scale, active, target, tsum, pbias, pieces):
    keys = tuple(pieces)
    tokens, width = target.shape
    hidden = active.shape[1]
    whole = pl.BlockSpec(memory_space=VMEM)
    smem = pl.BlockSpec(memory_space=SMEM)
    return pl.pallas_call(
        functools.partial(grad_kernel, keys),
        in_specs=[smem, smem] + [whole] * (4 + len(keys)),
        out_specs=[whole, whole],
        out_shape=[jax.ShapeDtypeStruct((hidden, width), bf16), jax.ShapeDtypeStruct((tokens, width), bf16)],
        scratch_shapes=[pltpu.VMEM((tokens, width), f32), pltpu.VMEM((tokens, 128), f32), pltpu.VMEM((tokens, 128), f32)],
        compiler_params=params(48),
        cost_estimate=cost(2 * tokens * hidden * width, 20 * MIB),
        name="weight_and_grad",
    )(place, scale, active, target, tsum, pbias.reshape(1, -1), *[pieces[key] for key in keys])


def outer_kernel(act_ref, grad_ref, out_ref):
    out_ref[...] = jnp.dot(act_ref[...], grad_ref[...], preferred_element_type=f32).astype(out_ref.dtype)


def outer(rows, grad, start, count, dtype):
    tokens, width = grad.shape
    step = 256
    first = start // step
    return pl.pallas_call(
        outer_kernel,
        grid=(count // step,),
        in_specs=[
            pl.BlockSpec((step, tokens), lambda i: (first + i, 0)),
            pl.BlockSpec((tokens, width), lambda i: (0, 0)),
        ],
        out_specs=pl.BlockSpec((step, width), lambda i: (i, 0)),
        out_shape=jax.ShapeDtypeStruct((count, width), dtype),
        compiler_params=params(24, 1),
        cost_estimate=cost(2 * count * tokens * width, 8 * MIB),
        name="outer",
    )(rows, grad)


def pre_kernel(grad_ref, w_ref, pre_ref, out_ref):
    back = lax.dot_general(grad_ref[...], w_ref[...], (((1,), (1,)), ((), ())), preferred_element_type=f32)
    p = pre_ref[...].astype(f32)
    s = jax.nn.sigmoid(p)
    out_ref[...] = (back * (s * (1.0 + p * (1.0 - s)))).astype(bf16)


def pre_grads(grad, weight, pre):
    tokens, width = grad.shape
    hidden = weight.shape[0]
    step = 256
    return pl.pallas_call(
        pre_kernel,
        grid=(hidden // step,),
        in_specs=[
            pl.BlockSpec((tokens, width), lambda i: (0, 0)),
            pl.BlockSpec((step, width), lambda i: (i, 0)),
            pl.BlockSpec((tokens, step), lambda i: (0, i)),
        ],
        out_specs=pl.BlockSpec((tokens, step), lambda i: (0, i)),
        out_shape=jax.ShapeDtypeStruct((tokens, hidden), bf16),
        compiler_params=params(24, 1),
        cost_estimate=cost(2 * tokens * hidden * width, 14 * MIB),
        name="pre_grads",
    )(grad, weight, pre)


def sum_over_z(block):
    count = 8
    width = block.shape[1]
    me = lax.axis_index("z")
    parts = block.reshape(count, 8, width)
    parts = lax.dynamic_slice_in_dim(jnp.concatenate([parts, parts], axis=0).astype(bf16), me, count, axis=0)
    total = lax.dynamic_slice_in_dim(block.reshape(count, 8, width), me, 1, axis=0)[0]
    for step in range(1, count):
        total = total + shift(parts[step], "z", step).astype(f32)
    mine = total.astype(bf16)
    got = [mine] + [shift(mine, "z", -step) for step in range(1, count)]
    got = jnp.stack(got, axis=0)
    back = (count - me) % count
    got = lax.dynamic_slice_in_dim(jnp.concatenate([got, got], axis=0), back, count, axis=0)
    return got.reshape(block.shape).astype(f32)


def body(features, enc_gain, enc_bias, row_source, timesteps, pre_act, proj_weight, proj_bias):
    place = jnp.stack([lax.axis_index("y"), lax.axis_index("x"), lax.axis_index("c")]).astype(jnp.int32)
    pre = pre_act.reshape(-1, pre_act.shape[-1])
    halves = gather_weight(proj_weight)
    pieces = {}
    for kind in range(2):
        for offset in range(4):
            for half in range(2):
                pieces[(0, kind, offset, half)] = halves[kind][offset][half]
                pieces[(1, kind, offset, half)] = shift(halves[kind][offset][half], "c", 1)
    left = shift(features[:, 1:], "z", 1)
    right = shift(features[:, :2], "z", -1)
    local_low = row_source - (lax.axis_index("z") * 3 - 2)
    rows = hidden_rows(place, pre)
    active = jax.nn.silu(pre.astype(f32)).astype(bf16)
    target, tsum = make_target(local_low, left, features, right, enc_gain, enc_bias)
    scale = 1.0 - timesteps.astype(f32) / 1000.0
    weight, grad = weight_and_grad(place, scale, active, target, tsum, proj_bias, pieces)
    away = outer(rows, grad, 1024, 1024, bf16)
    kept = outer(rows, grad, 0, 1024, f32)
    from_core = shift(away, "c", 1)
    both = kept + from_core.astype(f32)
    tops = []
    for kind, (first, second) in enumerate((("x", "y"), ("y", "x"))):
        part = both[kind * 512 : kind * 512 + 512].reshape(4, 2, 64, -1)
        top, bottom = scatter_ring([(part[d, 0], part[d, 1]) for d in range(4)], first)
        part = [top[:32], top[32:], bottom[:32], bottom[32:]]
        top, bottom = scatter_ring([(block[:16], block[16:]) for block in part], second)
        tops += [top, bottom]
    weight_grad = sum_over_z(jnp.concatenate(tops, axis=0))
    pre_grad = pre_grads(grad, weight, pre)
    return (pre_grad.reshape(pre_act.shape), weight_grad)


def solution(mesh):
    fine = Mesh(mesh.devices.reshape(4, 4, 2, 8), ("y", "x", "c", "z"))
    dp = ("y", "x", "c")
    return jax.shard_map(
        body,
        mesh=fine,
        in_specs=(
            P(dp, "z", None, None),
            P(),
            P(),
            P(dp, "z"),
            P(dp),
            P(dp, "z", None, None),
            P(dp, None),
            P(),
        ),
        out_specs=(P(dp, "z", None, None), P(dp, None)),
        check_vma=False,
    )
```

```python
import functools

import jax
import jax.numpy as jnp
from jax import lax
from jax.experimental import pallas as pl
from jax.experimental.pallas import tpu as pltpu
from jax.sharding import Mesh, PartitionSpec as P

loss_scale = 1024.0
norm_eps = 1e-06
MIB = 1 << 20
bf16, f32 = jnp.bfloat16, jnp.float32
VMEM = pltpu.VMEM
SMEM = pltpu.SMEM


def shift(block, axis, step):
    count = lax.axis_size(axis)
    return lax.ppermute(block, axis, [(i, (i + step) % count) for i in range(count)])


def turn(block, order, step):
    pairs = []
    for y in range(4):
        for x in range(4):
            for c in range(2):
                along_x = (c == 0) == (order == 0)
                to_y, to_x = (y, (x + step) % 4) if along_x else ((y + step) % 4, x)
                pairs.append(((y * 4 + x) * 2 + c, (to_y * 4 + to_x) * 2 + c))
    return lax.ppermute(block, ("y", "x", "c"), pairs)


FIRST, SECOND = 0, 1
LINE = (0, 3, 1, 2)
ORDER = (2, 1, 3, 0)


def params(mib, steps=0):
    semantics = ("arbitrary",) * steps if steps else None
    return pltpu.CompilerParams(vmem_limit_bytes=mib * MIB, dimension_semantics=semantics)


def cost(flops, nbytes, trans=0):
    return pl.CostEstimate(flops=flops // 64, bytes_accessed=nbytes // 64, transcendentals=trans // 64)


def gate_kernel(*refs):
    pass


def gate(arrays, after):
    anywhere = pl.BlockSpec(memory_space=pl.ANY)
    return pl.pallas_call(
        gate_kernel,
        in_specs=[anywhere] * (len(arrays) + len(after)),
        out_specs=[anywhere] * len(arrays),
        out_shape=[jax.ShapeDtypeStruct(array.shape, array.dtype) for array in arrays],
        input_output_aliases={k: k for k in range(len(arrays))},
        compiler_params=params(1),
        cost_estimate=cost(0, 0),
        name="gate",
    )(*arrays, *after)


def pack_kernel(own_ref, left_ref, right_ref, far_ref, after_ref, out_ref):
    for k, ref in enumerate((own_ref, left_ref, right_ref, far_ref)):
        out_ref[k * 64 : k * 64 + 64, :] = ref[...]


def pack(own, left, right, far, after):
    whole = pl.BlockSpec(memory_space=VMEM)
    return pl.pallas_call(
        pack_kernel,
        in_specs=[whole] * 4 + [pl.BlockSpec(memory_space=pl.ANY)],
        out_specs=whole,
        out_shape=jax.ShapeDtypeStruct((256, own.shape[1]), bf16),
        compiler_params=params(4),
        cost_estimate=cost(0, MIB),
        name="pack",
    )(own, left, right, far, after)


def spot_of(core, second, first, my_y, my_x):
    y = jnp.where(core == 0, my_y + second, my_y + first) % 4
    x = jnp.where(core == 0, my_x + first, my_x + second) % 4
    return y * 4 + x


def here():
    return lax.axis_index("y"), lax.axis_index("x"), lax.axis_index("c")


def silu_kernel(pre_ref, rows_ref, act_ref):
    step = pl.program_id(0)
    my_y, my_x, my_c = here()
    dy = (step // 4 - my_y + 4) % 4
    dx = (step % 4 - my_x + 4) % 4
    p = pre_ref[...].astype(f32)
    active = (p * jax.nn.sigmoid(p)).astype(bf16)
    turned = active.T
    for c in range(2):
        dc = (c - my_c + 2) % 2
        second, first = (dy, dx) if c == 0 else (dx, dy)
        block = jnp.where(second == 2, 0, jnp.where(second == 0, 3, jnp.where(second == 1, 1, 2)))
        spot = jnp.where(first == 0, 0, jnp.where(first == 3, 1, first + 1))
        row = pl.multiple_of(dc * 1024 + block * 256 + spot * 64, 64)
        rows_ref[pl.ds(row, 64), :] = turned[c * 64 : c * 64 + 64, :]

    @pl.when(step == pl.num_programs(0) - 1)
    def _():
        for at, k in enumerate((0, 1, 8, 9, 2, 3, 4, 5, 6, 7, 10, 11, 12, 13, 14, 15)):
            act_ref[:, at * 128 : at * 128 + 128] = rows_ref[k * 128 : k * 128 + 128, :].T


def hidden_rows(pre):
    tokens, hidden = pre.shape
    return pl.pallas_call(
        silu_kernel,
        grid=(hidden // 128,),
        in_specs=[pl.BlockSpec((tokens, 128), lambda i: (0, i))],
        out_specs=[
            pl.BlockSpec((hidden, tokens), lambda i: (0, 0)),
            pl.BlockSpec((tokens, hidden), lambda i: (0, 0)),
        ],
        out_shape=[jax.ShapeDtypeStruct((hidden, tokens), bf16), jax.ShapeDtypeStruct((tokens, hidden), bf16)],
        compiler_params=params(20, 1),
        cost_estimate=cost(tokens * hidden * 8, tokens * hidden * 6, tokens * hidden),
        name="hidden_rows",
    )(pre)


def target_kernel(source_ref, left_ref, mid_ref, right_ref, gain_ref, bias_ref, after_ref, out_ref, sum_ref, ext_ref):
    gain, bias = gain_ref[...].reshape(1, -1), bias_ref[...].reshape(1, -1)
    width = gain.shape[-1]
    offset = lax.axis_index("z") * 3 - 2
    for b in range(2):
        row = 0
        for ref, count in ((left_ref, 2), (mid_ref, 3), (right_ref, 2)):
            for k in range(count):
                x = ref[b, k].astype(f32)
                center = x - jnp.sum(x, axis=-1, keepdims=True) * (1.0 / width)
                spread = jnp.sum(center * center, axis=-1, keepdims=True) * (1.0 / width)
                ext_ref[b, row : row + 32, :] = (center * lax.rsqrt(spread + norm_eps) * gain + bias).astype(bf16)
                row += 32
    c = lax.broadcasted_iota(jnp.int32, (64, 224), 0)
    lane = lax.broadcasted_iota(jnp.int32, (64, 224), 1)
    source, j = lane // 32, lane % 32
    odd = c % 2 == 1
    low = jnp.where(odd, (c - 1) // 2, c // 2 - 1)
    high_w = jnp.where(odd, 0.25, 0.75).astype(f32)
    columns = jnp.where(j == jnp.clip(low, 0, 31), 1.0 - high_w, 0.0) + jnp.where(
        j == jnp.clip(low + 1, 0, 31), high_w, 0.0
    )
    for b in range(2):
        for r in range(6):
            h = 0.25 if r % 2 == 1 else 0.75
            first = source_ref[b, r] - offset
            rows = jnp.where(source == first, 1.0 - h, 0.0) + jnp.where(source == first + 1, h, 0.0)
            blend = (columns * rows).astype(bf16)
            target = jnp.dot(blend, ext_ref[b], preferred_element_type=f32)
            at = (b * 6 + r) * 64
            out_ref[at : at + 64, :] = target
            sum_ref[at : at + 64, :] = jnp.broadcast_to(jnp.sum(target * target, axis=-1, keepdims=True), (64, 128))


def make_target(row_source, left, mid, right, gain, bias, after):
    width = gain.shape[-1]
    whole = pl.BlockSpec(memory_space=VMEM)
    return pl.pallas_call(
        target_kernel,
        in_specs=[pl.BlockSpec(memory_space=SMEM)] + [whole] * 5 + [pl.BlockSpec(memory_space=pl.ANY)],
        out_specs=[whole, whole],
        out_shape=[jax.ShapeDtypeStruct((768, width), f32), jax.ShapeDtypeStruct((768, 128), f32)],
        scratch_shapes=[pltpu.VMEM((2, 224, width), bf16)],
        compiler_params=params(16),
        cost_estimate=cost(2 * 768 * 224 * width, 768 * width * 8),
        name="make_target",
    )(row_source, left, mid, right, gain, bias, after)


def near_kernel(first, has_base, act_ref, base_ref, *refs):
    pieces, (out_ref, w_ref, sem_ref) = refs[:3], refs[-3:]
    copies = [
        pltpu.make_async_copy(piece_ref, w_ref.at[k * 256 : k * 256 + 256], sem_ref.at[k])
        for k, piece_ref in enumerate(pieces)
    ]
    for copy in copies:
        copy.start()
    for copy in copies:
        copy.wait()
    step = 256
    for n in range(out_ref.shape[1] // step):
        at = slice(n * step, n * step + step)
        base = base_ref[:, at] if has_base else base_ref[at].reshape(1, -1)
        out_ref[:, at] = base + jnp.dot(act_ref[:, first : first + 768], w_ref[:, at], preferred_element_type=f32)


def near_part(active, base, pieces, first, after):
    tokens = active.shape[0]
    width = base.shape[-1]
    whole = pl.BlockSpec(memory_space=VMEM)
    anywhere = pl.BlockSpec(memory_space=pl.ANY)
    return pl.pallas_call(
        functools.partial(near_kernel, first, base.ndim == 2),
        in_specs=[whole] * 2 + [anywhere] * 4,
        out_specs=whole,
        out_shape=jax.ShapeDtypeStruct((tokens, width), f32),
        scratch_shapes=[pltpu.VMEM((768, width), bf16), pltpu.SemaphoreType.DMA((3,))],
        compiler_params=params(12),
        cost_estimate=cost(2 * tokens * 768 * width, 8 * MIB),
        name="near_part",
    )(active, base, *pieces, after)


def grad_kernel(time_ref, near_ref, act_ref, target_ref, tsum_ref, *refs):
    pieces, (out_ref, proj_ref, pp_ref, pt_ref, w_ref, sem_ref) = refs[:4], refs[4:]
    copies = [
        pltpu.make_async_copy(piece_ref, w_ref.at[k * 128 : k * 128 + 128], sem_ref.at[k])
        for k, piece_ref in enumerate(pieces)
    ]
    for copy in copies:
        copy.start()
    for copy in copies:
        copy.wait()
    width = out_ref.shape[1]
    step = 256
    pp_ref[...] = jnp.zeros_like(pp_ref)
    pt_ref[...] = jnp.zeros_like(pt_ref)

    for n in range(width // step):
        at = slice(n * step, n * step + step)
        proj = near_ref[:, at] + jnp.dot(act_ref[:, 0:512], w_ref[:, at], preferred_element_type=f32)
        proj_ref[:, at] = proj
        target = target_ref[:, at]
        square, cross = proj * proj, proj * target
        pp_ref[...] += square[:, :128] + square[:, 128:]
        pt_ref[...] += cross[:, :128] + cross[:, 128:]

    half_tokens = out_ref.shape[0] // 2
    for part in range(12):
        rows = slice(part * 64, part * 64 + 64)
        scaled = -loss_scale * (1.0 - time_ref[part * 64 // half_tokens].astype(f32) * 0.001)
        pn2 = jnp.sum(pp_ref[rows, :], axis=-1, keepdims=True) + norm_eps
        pt = jnp.sum(pt_ref[rows, :], axis=-1, keepdims=True)
        tn2 = tsum_ref[rows, 0:1] + norm_eps
        inv = lax.rsqrt(pn2) * lax.rsqrt(tn2)
        near = scaled * inv
        along = scaled * (pt * inv) / pn2
        out_ref[rows, :] = (near * target_ref[rows, :] - along * proj_ref[rows, :]).astype(bf16)


def out_grads(timesteps, near, active, target, tsum, pieces):
    tokens, width = target.shape
    whole = pl.BlockSpec(memory_space=VMEM)
    smem = pl.BlockSpec(memory_space=SMEM)
    return pl.pallas_call(
        grad_kernel,
        in_specs=[smem] + [whole] * 4 + [pl.BlockSpec(memory_space=pl.ANY)] * len(pieces),
        out_specs=whole,
        out_shape=jax.ShapeDtypeStruct((tokens, width), bf16),
        scratch_shapes=[
            pltpu.VMEM((tokens, width), f32),
            pltpu.VMEM((tokens, 128), f32),
            pltpu.VMEM((tokens, 128), f32),
            pltpu.VMEM((512, width), bf16),
            pltpu.SemaphoreType.DMA((4,)),
        ],
        compiler_params=params(20),
        cost_estimate=cost(2 * tokens * 512 * width, 15 * MIB),
        name="out_grads",
    )(timesteps, near, active, target, tsum, *pieces)


def outer_kernel(first, blocks, outs, added, *refs):
    rows_ref, grad_ref = refs[:2]
    extra_ref = refs[2] if added else None
    out_refs = refs[-len(outs) :]
    step = 256

    for n in range(grad_ref.shape[1] // step):
        at = slice(n * step, n * step + step)
        value = jnp.dot(rows_ref[first : first + blocks * 256, :], grad_ref[:, at], preferred_element_type=f32)
        if extra_ref is not None:
            value = value + extra_ref[:, at].astype(f32)
        for (start, count, dtype), out_ref in zip(outs, out_refs):
            out_ref[:, at] = value[start : start + count].astype(dtype)


def outer(rows, grad, start, count, outs, extra=None, after=None):
    tokens, width = grad.shape
    whole = pl.BlockSpec(memory_space=VMEM)
    inputs = [rows, grad] + ([] if extra is None else [extra])
    specs = [whole] * len(inputs)
    if after is not None:
        inputs, specs = inputs + [after], specs + [pl.BlockSpec(memory_space=pl.ANY)]
    return pl.pallas_call(
        functools.partial(outer_kernel, start, count // 256, outs, extra is not None),
        in_specs=specs,
        out_specs=[whole] * len(outs),
        out_shape=[jax.ShapeDtypeStruct((n, width), dtype) for _, n, dtype in outs],
        compiler_params=params(12),
        cost_estimate=cost(2 * count * tokens * width, 4 * MIB),
        name="outer",
    )(*inputs)


def whole_kernel(*refs):
    pieces, (w_ref, held_ref, sem_ref) = refs[:10], refs[-3:]
    my_y, my_x, my_c = here()
    copies, at, spots = [], 0, []
    for k, piece_ref in enumerate(pieces):
        count = piece_ref.shape[0]
        copies.append(pltpu.make_async_copy(piece_ref, held_ref.at[at : at + count], sem_ref.at[k]))
        at += count
    for copy in copies:
        copy.start()
    at = 0
    for copy, piece_ref in zip(copies, pieces):
        copy.wait()
        for _ in range(piece_ref.shape[0] // 64):
            core = (my_c + at // 1024) % 2
            row = spot_of(core, ORDER[at // 256 % 4], LINE[at // 64 % 4], my_y, my_x) * 128 + core * 64
            w_ref[pl.ds(pl.multiple_of(row, 64), 64), :] = held_ref[at : at + 64, :]
            at += 64


def whole_weight(pieces, after):
    width = pieces[0].shape[1]
    anywhere = pl.BlockSpec(memory_space=pl.ANY)
    return pl.pallas_call(
        whole_kernel,
        in_specs=[anywhere] * 11,
        out_specs=pl.BlockSpec(memory_space=VMEM),
        out_shape=jax.ShapeDtypeStruct((2048, width), bf16),
        scratch_shapes=[pltpu.VMEM((2048, width), bf16), pltpu.SemaphoreType.DMA((10,))],
        compiler_params=params(10),
        cost_estimate=cost(0, 12 * MIB),
        name="whole_weight",
    )(*pieces, after)


def pre_kernel(grad_ref, w_ref, pre_ref, *refs):
    out_ref = refs[-1]
    step = 256
    for k in range(pre_ref.shape[1] // step):
        at = slice(k * step, k * step + step)
        back = lax.dot_general(
            grad_ref[...], w_ref[at, :], (((1,), (1,)), ((), ())), preferred_element_type=f32
        )
        p = pre_ref[:, at].astype(f32)
        s = jax.nn.sigmoid(p)
        out_ref[:, at] = (back * (s * (1.0 + p * (1.0 - s)))).astype(bf16)


def pre_grads(grad, weight, pre, start, count, after, old=None):
    tokens, width = grad.shape
    hidden = weight.shape[0]
    step = 512
    first = start // step
    anywhere = pl.BlockSpec(memory_space=pl.ANY)
    inputs = [grad, weight, pre, after] + ([] if old is None else [old])
    block = pl.BlockSpec((tokens, step), lambda i: (0, first + i))
    return pl.pallas_call(
        pre_kernel,
        grid=(count // step,),
        in_specs=[
            pl.BlockSpec((tokens, width), lambda i: (0, 0)),
            pl.BlockSpec((step, width), lambda i: (first + i, 0)),
            block,
        ]
        + [anywhere] * (len(inputs) - 3),
        out_specs=block,
        out_shape=jax.ShapeDtypeStruct((tokens, hidden), bf16),
        input_output_aliases={} if old is None else {4: 0},
        compiler_params=params(20, 1),
        cost_estimate=cost(2 * tokens * count * width, 8 * MIB),
        name="pre_grads",
    )(*inputs)


def summed(own, blocks, axis):
    right, left, far = blocks
    return (
        own
        + turn(right, axis, 1).astype(f32)
        + turn(left, axis, -1).astype(f32)
        + turn(far, axis, 2).astype(f32)
    )


def body(features, enc_gain, enc_bias, row_source, timesteps, pre_act, proj_weight, proj_bias):
    width = proj_weight.shape[1]
    pre = pre_act.reshape(-1, pre_act.shape[-1])
    line = [proj_weight, turn(proj_weight, FIRST, 1), turn(proj_weight, FIRST, -1), turn(proj_weight, FIRST, 2)]
    left = shift(features[:, 1:], "z", 1)
    right = shift(features[:, :2], "z", -1)
    rows, active = hidden_rows(pre)
    line = pack(*line, rows)
    three, one = turn(line, SECOND, 1), turn(line, SECOND, -1)
    three, one = gate((three, one), (left, right))
    target, tsum = make_target(row_source, left, features, right, enc_gain, enc_bias, line)
    two = [turn(three[:128], SECOND, 1), turn(one[128:], SECOND, -1)]
    mine = [one, three, line]
    other = [shift(piece, "c", 1) for piece in mine]
    close = near_part(active, proj_bias, mine, 512, one)
    close = near_part(active, close, other, 1280, one)
    two = list(gate(two, (close, tsum)))
    other_two = [shift(piece, "c", 1) for piece in two]
    grad = out_grads(timesteps, close, active, target, tsum, two + other_two)
    (away_far,) = outer(rows, grad, 1024, 256, ((0, 256, bf16),))
    back_far = shift(away_far, "c", 1)
    (away,) = outer(rows, grad, 1280, 768, ((0, 768, bf16),), after=away_far)
    (away,) = gate((away,), (back_far,))
    back = shift(away, "c", 1)
    (far,) = outer(rows, grad, 0, 256, ((0, 256, bf16),), back_far, after=away)
    kept_outs = ((0, 256, bf16), (256, 256, bf16), (512, 256, f32))
    to_one, to_three, own = outer(rows, grad, 256, 768, kept_outs, back, after=far)
    weight = whole_weight(two + mine + other_two + other, to_one)
    pre_grad = pre_grads(grad, weight, pre, 0, 1536, to_three)
    (own,) = gate((own,), (pre_grad,))
    own = summed(own, (to_one, to_three, far), SECOND)
    blocks = {first: own[k * 64 : k * 64 + 64] for k, first in enumerate(LINE)}
    block = summed(blocks[0], [blocks[d].astype(bf16) for d in (1, 3, 2)], FIRST).astype(bf16)
    parts = lax.all_to_all(block, "z", 0, 0, tiled=True)
    pre_grad = pre_grads(grad, weight, pre, 1536, 512, block, pre_grad)
    (parts,) = gate((parts,), (pre_grad,))
    total = jnp.sum(parts.reshape(8, 8, width).astype(f32), axis=0).astype(bf16)
    total = jnp.broadcast_to(total[None], (8, 8, width)).reshape(block.shape)
    weight_grad = lax.all_to_all(total, "z", 0, 0, tiled=True).astype(f32)
    return (pre_grad.reshape(pre_act.shape), weight_grad)


def solution(mesh):
    fine = Mesh(mesh.devices.reshape(4, 4, 2, 8), ("y", "x", "c", "z"))
    dp = ("y", "x", "c")
    return jax.shard_map(
        body,
        mesh=fine,
        in_specs=(
            P(dp, "z", None, None),
            P(),
            P(),
            P(dp, "z"),
            P(dp),
            P(dp, "z", None, None),
            P(dp, None),
            P(),
        ),
        out_specs=(P(dp, "z", None, None), P(dp, None)),
        check_vma=False,
    )
```

```python
import functools

import jax
import jax.numpy as jnp
from jax import lax
from jax.experimental import pallas as pl
from jax.experimental.pallas import tpu as pltpu
from jax.sharding import Mesh, PartitionSpec as P

loss_scale = 1024.0
norm_eps = 1e-06
MIB = 1 << 20
bf16, f32 = jnp.bfloat16, jnp.float32
VMEM = pltpu.VMEM
SMEM = pltpu.SMEM


def shift(block, axis, step):
    count = lax.axis_size(axis)
    return lax.ppermute(block, axis, [(i, (i + step) % count) for i in range(count)])


def turn(block, order, step):
    pairs = []
    for y in range(4):
        for x in range(4):
            for c in range(2):
                along_x = (c == 0) == (order == 0)
                to_y, to_x = (y, (x + step) % 4) if along_x else ((y + step) % 4, x)
                pairs.append(((y * 4 + x) * 2 + c, (to_y * 4 + to_x) * 2 + c))
    return lax.ppermute(block, ("y", "x", "c"), pairs)


FIRST, SECOND = 0, 1
LINE = (0, 3, 1, 2)
ORDER = (2, 1, 3, 0)


def params(mib, steps=0):
    semantics = ("arbitrary",) * steps if steps else None
    return pltpu.CompilerParams(vmem_limit_bytes=mib * MIB, dimension_semantics=semantics)


def cost(flops, nbytes, trans=0):
    return pl.CostEstimate(flops=flops // 64, bytes_accessed=nbytes // 64, transcendentals=trans // 64)


def gate_kernel(*refs):
    pass


def gate(arrays, after):
    anywhere = pl.BlockSpec(memory_space=pl.ANY)
    return pl.pallas_call(
        gate_kernel,
        in_specs=[anywhere] * (len(arrays) + len(after)),
        out_specs=[anywhere] * len(arrays),
        out_shape=[jax.ShapeDtypeStruct(array.shape, array.dtype) for array in arrays],
        input_output_aliases={k: k for k in range(len(arrays))},
        compiler_params=params(1),
        cost_estimate=cost(0, 0),
        name="gate",
    )(*arrays, *after)


def pack_kernel(own_ref, left_ref, right_ref, far_ref, after_ref, out_ref):
    for k, ref in enumerate((own_ref, left_ref, right_ref, far_ref)):
        out_ref[k * 64 : k * 64 + 64, :] = ref[...]


def pack(own, left, right, far, after):
    whole = pl.BlockSpec(memory_space=VMEM)
    return pl.pallas_call(
        pack_kernel,
        in_specs=[whole] * 4 + [pl.BlockSpec(memory_space=pl.ANY)],
        out_specs=whole,
        out_shape=jax.ShapeDtypeStruct((256, own.shape[1]), bf16),
        compiler_params=params(4),
        cost_estimate=cost(0, MIB),
        name="pack",
    )(own, left, right, far, after)


def spot_of(core, second, first, my_y, my_x):
    y = jnp.where(core == 0, my_y + second, my_y + first) % 4
    x = jnp.where(core == 0, my_x + first, my_x + second) % 4
    return y * 4 + x


def here():
    return lax.axis_index("y"), lax.axis_index("x"), lax.axis_index("c")


def silu_kernel(pre_ref, rows_ref, act_ref):
    step = pl.program_id(0)
    my_y, my_x, my_c = here()
    dy = (step // 4 - my_y + 4) % 4
    dx = (step % 4 - my_x + 4) % 4
    p = pre_ref[...].astype(f32)
    active = (p * jax.nn.sigmoid(p)).astype(bf16)
    turned = active.T
    for c in range(2):
        dc = (c - my_c + 2) % 2
        second, first = (dy, dx) if c == 0 else (dx, dy)
        block = jnp.where(second == 2, 0, jnp.where(second == 0, 3, jnp.where(second == 1, 1, 2)))
        spot = jnp.where(first == 0, 0, jnp.where(first == 3, 1, first + 1))
        row = pl.multiple_of(dc * 1024 + block * 256 + spot * 64, 64)
        rows_ref[pl.ds(row, 64), :] = turned[c * 64 : c * 64 + 64, :]

    @pl.when(step == pl.num_programs(0) - 1)
    def _():
        for at, k in enumerate((6, 7, 14, 15, 2, 3, 4, 5, 0, 1, 10, 11, 12, 13, 8, 9)):
            act_ref[:, at * 128 : at * 128 + 128] = rows_ref[k * 128 : k * 128 + 128, :].T


def hidden_rows(pre):
    tokens, hidden = pre.shape
    return pl.pallas_call(
        silu_kernel,
        grid=(hidden // 128,),
        in_specs=[pl.BlockSpec((tokens, 128), lambda i: (0, i))],
        out_specs=[
            pl.BlockSpec((hidden, tokens), lambda i: (0, 0)),
            pl.BlockSpec((tokens, hidden), lambda i: (0, 0)),
        ],
        out_shape=[jax.ShapeDtypeStruct((hidden, tokens), bf16), jax.ShapeDtypeStruct((tokens, hidden), bf16)],
        compiler_params=params(20, 1),
        cost_estimate=cost(tokens * hidden * 8, tokens * hidden * 6, tokens * hidden),
        name="hidden_rows",
    )(pre)


def target_kernel(source_ref, left_ref, mid_ref, right_ref, gain_ref, bias_ref, after_ref, out_ref, sum_ref, ext_ref):
    gain, bias = gain_ref[...].reshape(1, -1), bias_ref[...].reshape(1, -1)
    width = gain.shape[-1]
    offset = lax.axis_index("z") * 3 - 2
    for b in range(2):
        row = 0
        for ref, count in ((left_ref, 2), (mid_ref, 3), (right_ref, 2)):
            for k in range(count):
                x = ref[b, k].astype(f32)
                center = x - jnp.sum(x, axis=-1, keepdims=True) * (1.0 / width)
                spread = jnp.sum(center * center, axis=-1, keepdims=True) * (1.0 / width)
                ext_ref[b, row : row + 32, :] = (center * lax.rsqrt(spread + norm_eps) * gain + bias).astype(bf16)
                row += 32
    c = lax.broadcasted_iota(jnp.int32, (64, 224), 0)
    lane = lax.broadcasted_iota(jnp.int32, (64, 224), 1)
    source, j = lane // 32, lane % 32
    odd = c % 2 == 1
    low = jnp.where(odd, (c - 1) // 2, c // 2 - 1)
    high_w = jnp.where(odd, 0.25, 0.75).astype(f32)
    columns = jnp.where(j == jnp.clip(low, 0, 31), 1.0 - high_w, 0.0) + jnp.where(
        j == jnp.clip(low + 1, 0, 31), high_w, 0.0
    )
    for b in range(2):
        for r in range(6):
            h = 0.25 if r % 2 == 1 else 0.75
            first = source_ref[b, r] - offset
            rows = jnp.where(source == first, 1.0 - h, 0.0) + jnp.where(source == first + 1, h, 0.0)
            blend = (columns * rows).astype(bf16)
            target = jnp.dot(blend, ext_ref[b], preferred_element_type=f32)
            at = (b * 6 + r) * 64
            out_ref[at : at + 64, :] = target
            sum_ref[at : at + 64, :] = jnp.broadcast_to(jnp.sum(target * target, axis=-1, keepdims=True), (64, 128))


def make_target(row_source, left, mid, right, gain, bias, after):
    width = gain.shape[-1]
    whole = pl.BlockSpec(memory_space=VMEM)
    return pl.pallas_call(
        target_kernel,
        in_specs=[pl.BlockSpec(memory_space=SMEM)] + [whole] * 5 + [pl.BlockSpec(memory_space=pl.ANY)],
        out_specs=[whole, whole],
        out_shape=[jax.ShapeDtypeStruct((768, width), f32), jax.ShapeDtypeStruct((768, 128), f32)],
        scratch_shapes=[pltpu.VMEM((2, 224, width), bf16)],
        compiler_params=params(16),
        cost_estimate=cost(2 * 768 * 224 * width, 768 * width * 8),
        name="make_target",
    )(row_source, left, mid, right, gain, bias, after)


def near_kernel(first, has_base, act_ref, base_ref, *refs):
    pieces, (out_ref, w_ref, sem_ref) = refs[:-4], refs[-3:]
    copies = [
        pltpu.make_async_copy(piece_ref, w_ref.at[k * 256 : k * 256 + 256], sem_ref.at[k])
        for k, piece_ref in enumerate(pieces)
    ]
    for copy in copies:
        copy.start()
    for copy in copies:
        copy.wait()
    step = 256
    for n in range(out_ref.shape[1] // step):
        at = slice(n * step, n * step + step)
        base = base_ref[:, at] if has_base else base_ref[at].reshape(1, -1)
        out_ref[:, at] = base + jnp.dot(act_ref[:, first : first + w_ref.shape[0]], w_ref[:, at], preferred_element_type=f32)


def near_part(active, base, pieces, first, after):
    tokens = active.shape[0]
    width = base.shape[-1]
    whole = pl.BlockSpec(memory_space=VMEM)
    anywhere = pl.BlockSpec(memory_space=pl.ANY)
    return pl.pallas_call(
        functools.partial(near_kernel, first, base.ndim == 2),
        in_specs=[whole] * 2 + [anywhere] * (len(pieces) + 1),
        out_specs=whole,
        out_shape=jax.ShapeDtypeStruct((tokens, width), f32),
        scratch_shapes=[pltpu.VMEM((256 * len(pieces), width), bf16), pltpu.SemaphoreType.DMA((len(pieces),))],
        compiler_params=params(12),
        cost_estimate=cost(2 * tokens * 768 * width, 8 * MIB),
        name="near_part",
    )(active, base, *pieces, after)


def grad_kernel(time_ref, near_ref, act_ref, target_ref, tsum_ref, *refs):
    pieces, (out_ref, proj_ref, pp_ref, pt_ref, w_ref, sem_ref) = refs[:1], refs[1:]
    copies = [
        pltpu.make_async_copy(piece_ref, w_ref.at[k * 256 : k * 256 + 256], sem_ref.at[k])
        for k, piece_ref in enumerate(pieces)
    ]
    for copy in copies:
        copy.start()
    for copy in copies:
        copy.wait()
    width = out_ref.shape[1]
    step = 256
    pp_ref[...] = jnp.zeros_like(pp_ref)
    pt_ref[...] = jnp.zeros_like(pt_ref)

    for n in range(width // step):
        at = slice(n * step, n * step + step)
        proj = near_ref[:, at] + jnp.dot(act_ref[:, 1792:2048], w_ref[:, at], preferred_element_type=f32)
        proj_ref[:, at] = proj
        target = target_ref[:, at]
        square, cross = proj * proj, proj * target
        pp_ref[...] += square[:, :128] + square[:, 128:]
        pt_ref[...] += cross[:, :128] + cross[:, 128:]

    half_tokens = out_ref.shape[0] // 2
    for part in range(12):
        rows = slice(part * 64, part * 64 + 64)
        scaled = -loss_scale * (1.0 - time_ref[part * 64 // half_tokens].astype(f32) * 0.001)
        pn2 = jnp.sum(pp_ref[rows, :], axis=-1, keepdims=True) + norm_eps
        pt = jnp.sum(pt_ref[rows, :], axis=-1, keepdims=True)
        tn2 = tsum_ref[rows, 0:1] + norm_eps
        inv = lax.rsqrt(pn2) * lax.rsqrt(tn2)
        near = scaled * inv
        along = scaled * (pt * inv) / pn2
        out_ref[rows, :] = (near * target_ref[rows, :] - along * proj_ref[rows, :]).astype(bf16)


def out_grads(timesteps, near, active, target, tsum, pieces):
    tokens, width = target.shape
    whole = pl.BlockSpec(memory_space=VMEM)
    smem = pl.BlockSpec(memory_space=SMEM)
    return pl.pallas_call(
        grad_kernel,
        in_specs=[smem] + [whole] * 4 + [pl.BlockSpec(memory_space=pl.ANY)] * len(pieces),
        out_specs=whole,
        out_shape=jax.ShapeDtypeStruct((tokens, width), bf16),
        scratch_shapes=[
            pltpu.VMEM((tokens, width), f32),
            pltpu.VMEM((tokens, 128), f32),
            pltpu.VMEM((tokens, 128), f32),
            pltpu.VMEM((256, width), bf16),
            pltpu.SemaphoreType.DMA((1,)),
        ],
        compiler_params=params(20),
        cost_estimate=cost(2 * tokens * 512 * width, 15 * MIB),
        name="out_grads",
    )(timesteps, near, active, target, tsum, *pieces)


def outer_kernel(first, blocks, outs, added, *refs):
    rows_ref, grad_ref = refs[:2]
    extra_ref = refs[2] if added else None
    out_refs = refs[-len(outs) :]
    step = 256

    for n in range(grad_ref.shape[1] // step):
        at = slice(n * step, n * step + step)
        value = jnp.dot(rows_ref[first : first + blocks * 256, :], grad_ref[:, at], preferred_element_type=f32)
        if extra_ref is not None:
            value = value + extra_ref[:, at].astype(f32)
        for (start, count, dtype), out_ref in zip(outs, out_refs):
            out_ref[:, at] = value[start : start + count].astype(dtype)


def outer(rows, grad, start, count, outs, extra=None, after=None):
    tokens, width = grad.shape
    whole = pl.BlockSpec(memory_space=VMEM)
    inputs = [rows, grad] + ([] if extra is None else [extra])
    specs = [whole] * len(inputs)
    if after is not None:
        inputs, specs = inputs + [after], specs + [pl.BlockSpec(memory_space=pl.ANY)]
    return pl.pallas_call(
        functools.partial(outer_kernel, start, count // 256, outs, extra is not None),
        in_specs=specs,
        out_specs=[whole] * len(outs),
        out_shape=[jax.ShapeDtypeStruct((n, width), dtype) for _, n, dtype in outs],
        compiler_params=params(12),
        cost_estimate=cost(2 * count * tokens * width, 4 * MIB),
        name="outer",
    )(*inputs)


def whole_kernel(*refs):
    pieces, (w_ref, held_ref, sem_ref) = refs[:8], refs[-3:]
    my_y, my_x, my_c = here()
    copies, at, spots = [], 0, []
    for k, piece_ref in enumerate(pieces):
        count = piece_ref.shape[0]
        copies.append(pltpu.make_async_copy(piece_ref, held_ref.at[at : at + count], sem_ref.at[k]))
        at += count
    for copy in copies:
        copy.start()
    at = 0
    for copy, piece_ref in zip(copies, pieces):
        copy.wait()
        for _ in range(piece_ref.shape[0] // 64):
            core = (my_c + at // 1024) % 2
            row = spot_of(core, ORDER[at // 256 % 4], LINE[at // 64 % 4], my_y, my_x) * 128 + core * 64
            w_ref[pl.ds(pl.multiple_of(row, 64), 64), :] = held_ref[at : at + 64, :]
            at += 64


def whole_weight(pieces, after):
    width = pieces[0].shape[1]
    anywhere = pl.BlockSpec(memory_space=pl.ANY)
    return pl.pallas_call(
        whole_kernel,
        in_specs=[anywhere] * 9,
        out_specs=pl.BlockSpec(memory_space=VMEM),
        out_shape=jax.ShapeDtypeStruct((2048, width), bf16),
        scratch_shapes=[pltpu.VMEM((2048, width), bf16), pltpu.SemaphoreType.DMA((8,))],
        compiler_params=params(10),
        cost_estimate=cost(0, 12 * MIB),
        name="whole_weight",
    )(*pieces, after)


def pre_kernel(grad_ref, w_ref, pre_ref, *refs):
    out_ref, token_ref = refs[-2:]
    step = 256
    for k in range(pre_ref.shape[1] // step):
        at = slice(k * step, k * step + step)
        back = lax.dot_general(
            grad_ref[...], w_ref[at, :], (((1,), (1,)), ((), ())), preferred_element_type=f32
        )
        p = pre_ref[:, at].astype(f32)
        s = jax.nn.sigmoid(p)
        out_ref[:, at] = (back * (s * (1.0 + p * (1.0 - s)))).astype(bf16)
    token_ref[...] = jnp.zeros_like(token_ref)


def pre_grads(grad, weight, pre, first, count, after, old=None):
    tokens, width = grad.shape
    hidden = weight.shape[0]
    step = 512
    block = pl.BlockSpec((tokens, step), lambda i: (0, first + i))
    anywhere = pl.BlockSpec(memory_space=pl.ANY)
    inputs = [grad, weight, pre, after] + ([] if old is None else [old])
    return pl.pallas_call(
        pre_kernel,
        grid=(count,),
        in_specs=[
            pl.BlockSpec((tokens, width), lambda i: (0, 0)),
            pl.BlockSpec((step, width), lambda i: (first + i, 0)),
            block,
        ]
        + [anywhere] * (len(inputs) - 3),
        out_specs=[block, pl.BlockSpec((8, 128), lambda i: (0, 0))],
        out_shape=[jax.ShapeDtypeStruct((tokens, hidden), bf16), jax.ShapeDtypeStruct((8, 128), f32)],
        input_output_aliases={} if old is None else {4: 0},
        compiler_params=params(20, 1),
        cost_estimate=cost(2 * tokens * step * count * width, 4 * MIB * count),
        name="pre_grads",
    )(*inputs)


def summed(own, blocks, axis):
    right, left, far = blocks
    return (
        own
        + turn(right, axis, 1).astype(f32)
        + turn(left, axis, -1).astype(f32)
        + turn(far, axis, 2).astype(f32)
    )


def body(features, enc_gain, enc_bias, row_source, timesteps, pre_act, proj_weight, proj_bias):
    width = proj_weight.shape[1]
    pre = pre_act.reshape(-1, pre_act.shape[-1])
    line = [proj_weight, turn(proj_weight, FIRST, 1), turn(proj_weight, FIRST, -1), turn(proj_weight, FIRST, 2)]
    rows, active = hidden_rows(pre)
    line = pack(*line, rows)
    three, one, two = turn(line, SECOND, 1), turn(line, SECOND, -1), turn(line, SECOND, 2)
    other_line = shift(line, "c", 1)
    left, right = gate((features[:, 1:], features[:, :2]), (other_line,))
    left, right = shift(left, "z", 1), shift(right, "z", -1)
    target, tsum = make_target(row_source, left, features, right, enc_gain, enc_bias, line)
    close = near_part(active, proj_bias, [line, other_line], 0, line)
    mine = list(gate((two, one, three), (close, tsum)))
    other = [shift(piece, "c", 1) for piece in mine]
    close = near_part(active, close, mine[1:] + mine[:1], 512, line)
    close = near_part(active, close, other[1:], 1280, line)
    grad = out_grads(timesteps, close, active, target, tsum, other[:1])
    mine, other = mine + [line], other + [other_line]
    (away_far,) = outer(rows, grad, 1024, 256, ((0, 256, bf16),))
    back_far = shift(away_far, "c", 1)
    (away,) = outer(rows, grad, 1280, 768, ((0, 768, bf16),), after=away_far)
    (away,) = gate((away,), (back_far,))
    back = shift(away, "c", 1)
    (far,) = outer(rows, grad, 0, 256, ((0, 256, bf16),), back_far, after=away)
    kept_outs = ((0, 256, bf16), (256, 256, bf16), (512, 256, f32))
    to_one, to_three, own = outer(rows, grad, 256, 768, kept_outs, back, after=far)
    weight = whole_weight(mine + other, to_one)
    pre_grad, token = pre_grads(grad, weight, pre, 0, 3, to_three)
    (own,) = gate((own,), (token,))
    own = summed(own, (to_one, to_three, far), SECOND)
    blocks = {first: own[k * 64 : k * 64 + 64] for k, first in enumerate(LINE)}
    pre_grad, token = pre_grads(grad, weight, pre, 3, 1, own, pre_grad)
    (kept,) = gate((blocks[0],), (token,))
    block = summed(kept, [blocks[d].astype(bf16) for d in (1, 3, 2)], FIRST).astype(bf16)
    parts = lax.all_to_all(block, "z", 0, 0, tiled=True)
    total = jnp.sum(parts.reshape(8, 8, width).astype(f32), axis=0).astype(bf16)
    total = jnp.broadcast_to(total[None], (8, 8, width)).reshape(block.shape)
    weight_grad = lax.all_to_all(total, "z", 0, 0, tiled=True).astype(f32)
    return (pre_grad.reshape(pre_act.shape), weight_grad)


def solution(mesh):
    fine = Mesh(mesh.devices.reshape(4, 4, 2, 8), ("y", "x", "c", "z"))
    dp = ("y", "x", "c")
    return jax.shard_map(
        body,
        mesh=fine,
        in_specs=(
            P(dp, "z", None, None),
            P(),
            P(),
            P(dp, "z"),
            P(dp),
            P(dp, "z", None, None),
            P(dp, None),
            P(),
        ),
        out_specs=(P(dp, "z", None, None), P(dp, None)),
        check_vma=False,
    )
```

```python
import functools

import jax
import jax.numpy as jnp
from jax import lax
from jax.experimental import pallas as pl
from jax.experimental.pallas import tpu as pltpu
from jax.sharding import Mesh, PartitionSpec as P

loss_scale = 1024.0
norm_eps = 1e-06
MIB = 1 << 20
bf16, f32 = jnp.bfloat16, jnp.float32
VMEM = pltpu.VMEM
SMEM = pltpu.SMEM


def shift(block, axis, step):
    count = lax.axis_size(axis)
    return lax.ppermute(block, axis, [(i, (i + step) % count) for i in range(count)])


def turn(block, order, step):
    pairs = []
    for y in range(4):
        for x in range(4):
            for c in range(2):
                along_x = (c == 0) == (order == 0)
                to_y, to_x = (y, (x + step) % 4) if along_x else ((y + step) % 4, x)
                pairs.append(((y * 4 + x) * 2 + c, (to_y * 4 + to_x) * 2 + c))
    return lax.ppermute(block, ("y", "x", "c"), pairs)


FIRST, SECOND = 0, 1
LINE = (0, 3, 1, 2)
ORDER = (2, 1, 3, 0)


def params(mib, steps=0):
    semantics = ("arbitrary",) * steps if steps else None
    return pltpu.CompilerParams(vmem_limit_bytes=mib * MIB, dimension_semantics=semantics)


def cost(flops, nbytes, trans=0):
    return pl.CostEstimate(flops=flops // 64, bytes_accessed=nbytes // 64, transcendentals=trans // 64)


def gate_kernel(*refs):
    pass


def gate(arrays, after):
    anywhere = pl.BlockSpec(memory_space=pl.ANY)
    return pl.pallas_call(
        gate_kernel,
        in_specs=[anywhere] * (len(arrays) + len(after)),
        out_specs=[anywhere] * len(arrays),
        out_shape=[jax.ShapeDtypeStruct(array.shape, array.dtype) for array in arrays],
        input_output_aliases={k: k for k in range(len(arrays))},
        compiler_params=params(1),
        cost_estimate=cost(0, 0),
        name="gate",
    )(*arrays, *after)


def pack_kernel(own_ref, left_ref, right_ref, far_ref, after_ref, out_ref):
    for k, ref in enumerate((own_ref, left_ref, right_ref, far_ref)):
        out_ref[k * 64 : k * 64 + 64, :] = ref[...]


def pack(own, left, right, far, after):
    whole = pl.BlockSpec(memory_space=VMEM)
    return pl.pallas_call(
        pack_kernel,
        in_specs=[whole] * 4 + [pl.BlockSpec(memory_space=pl.ANY)],
        out_specs=whole,
        out_shape=jax.ShapeDtypeStruct((256, own.shape[1]), bf16),
        compiler_params=params(4),
        cost_estimate=cost(0, MIB),
        name="pack",
    )(own, left, right, far, after)


def spot_of(core, second, first, my_y, my_x):
    y = jnp.where(core == 0, my_y + second, my_y + first) % 4
    x = jnp.where(core == 0, my_x + first, my_x + second) % 4
    return y * 4 + x


def here():
    return lax.axis_index("y"), lax.axis_index("x"), lax.axis_index("c")


def silu_kernel(pre_ref, rows_ref, act_ref):
    step = pl.program_id(0)
    my_y, my_x, my_c = here()
    dy = (step // 4 - my_y + 4) % 4
    dx = (step % 4 - my_x + 4) % 4
    p = pre_ref[...].astype(f32)
    active = (p * jax.nn.sigmoid(p)).astype(bf16)
    turned = active.T
    for c in range(2):
        dc = (c - my_c + 2) % 2
        second, first = (dy, dx) if c == 0 else (dx, dy)
        block = jnp.where(second == 2, 0, jnp.where(second == 0, 3, jnp.where(second == 1, 1, 2)))
        spot = jnp.where(first == 0, 0, jnp.where(first == 3, 1, first + 1))
        row = pl.multiple_of(dc * 1024 + block * 256 + spot * 64, 64)
        rows_ref[pl.ds(row, 64), :] = turned[c * 64 : c * 64 + 64, :]

    @pl.when(step == pl.num_programs(0) - 1)
    def _():
        for at, k in enumerate((6, 7, 14, 15, 2, 3, 4, 5, 0, 1, 10, 11, 12, 13, 8, 9)):
            act_ref[:, at * 128 : at * 128 + 128] = rows_ref[k * 128 : k * 128 + 128, :].T


def hidden_rows(pre):
    tokens, hidden = pre.shape
    return pl.pallas_call(
        silu_kernel,
        grid=(hidden // 128,),
        in_specs=[pl.BlockSpec((tokens, 128), lambda i: (0, i))],
        out_specs=[
            pl.BlockSpec((hidden, tokens), lambda i: (0, 0)),
            pl.BlockSpec((tokens, hidden), lambda i: (0, 0)),
        ],
        out_shape=[jax.ShapeDtypeStruct((hidden, tokens), bf16), jax.ShapeDtypeStruct((tokens, hidden), bf16)],
        compiler_params=params(20, 1),
        cost_estimate=cost(tokens * hidden * 8, tokens * hidden * 6, tokens * hidden),
        name="hidden_rows",
    )(pre)


def target_kernel(source_ref, left_ref, mid_ref, right_ref, gain_ref, bias_ref, after_ref, out_ref, sum_ref, ext_ref):
    gain, bias = gain_ref[...].reshape(1, -1), bias_ref[...].reshape(1, -1)
    width = gain.shape[-1]
    offset = lax.axis_index("z") * 3 - 2
    for b in range(2):
        row = 0
        for ref, count in ((left_ref, 2), (mid_ref, 3), (right_ref, 2)):
            for k in range(count):
                x = ref[b, k].astype(f32)
                center = x - jnp.sum(x, axis=-1, keepdims=True) * (1.0 / width)
                spread = jnp.sum(center * center, axis=-1, keepdims=True) * (1.0 / width)
                ext_ref[b, row : row + 32, :] = (center * lax.rsqrt(spread + norm_eps) * gain + bias).astype(bf16)
                row += 32
    c = lax.broadcasted_iota(jnp.int32, (64, 224), 0)
    lane = lax.broadcasted_iota(jnp.int32, (64, 224), 1)
    source, j = lane // 32, lane % 32
    odd = c % 2 == 1
    low = jnp.where(odd, (c - 1) // 2, c // 2 - 1)
    high_w = jnp.where(odd, 0.25, 0.75).astype(f32)
    columns = jnp.where(j == jnp.clip(low, 0, 31), 1.0 - high_w, 0.0) + jnp.where(
        j == jnp.clip(low + 1, 0, 31), high_w, 0.0
    )
    for b in range(2):
        for r in range(6):
            h = 0.25 if r % 2 == 1 else 0.75
            first = source_ref[b, r] - offset
            rows = jnp.where(source == first, 1.0 - h, 0.0) + jnp.where(source == first + 1, h, 0.0)
            blend = (columns * rows).astype(bf16)
            target = jnp.dot(blend, ext_ref[b], preferred_element_type=f32)
            at = (b * 6 + r) * 64
            out_ref[at : at + 64, :] = target
            sum_ref[at : at + 64, :] = jnp.broadcast_to(jnp.sum(target * target, axis=-1, keepdims=True), (64, 128))


def make_target(row_source, left, mid, right, gain, bias, after):
    width = gain.shape[-1]
    whole = pl.BlockSpec(memory_space=VMEM)
    return pl.pallas_call(
        target_kernel,
        in_specs=[pl.BlockSpec(memory_space=SMEM)] + [whole] * 5 + [pl.BlockSpec(memory_space=pl.ANY)],
        out_specs=[whole, whole],
        out_shape=[jax.ShapeDtypeStruct((768, width), f32), jax.ShapeDtypeStruct((768, 128), f32)],
        scratch_shapes=[pltpu.VMEM((2, 224, width), bf16)],
        compiler_params=params(16),
        cost_estimate=cost(2 * 768 * 224 * width, 768 * width * 8),
        name="make_target",
    )(row_source, left, mid, right, gain, bias, after)


def near_kernel(first, has_base, act_ref, base_ref, *refs):
    pieces, (out_ref, w_ref, sem_ref) = refs[:-4], refs[-3:]
    copies = [
        pltpu.make_async_copy(piece_ref, w_ref.at[k * 256 : k * 256 + 256], sem_ref.at[k])
        for k, piece_ref in enumerate(pieces)
    ]
    for copy in copies:
        copy.start()
    for copy in copies:
        copy.wait()
    step = 256
    for n in range(out_ref.shape[1] // step):
        at = slice(n * step, n * step + step)
        base = base_ref[:, at] if has_base else base_ref[at].reshape(1, -1)
        out_ref[:, at] = base + jnp.dot(act_ref[:, first : first + w_ref.shape[0]], w_ref[:, at], preferred_element_type=f32)


def near_part(active, base, pieces, first, after):
    tokens = active.shape[0]
    width = base.shape[-1]
    whole = pl.BlockSpec(memory_space=VMEM)
    anywhere = pl.BlockSpec(memory_space=pl.ANY)
    return pl.pallas_call(
        functools.partial(near_kernel, first, base.ndim == 2),
        in_specs=[whole] * 2 + [anywhere] * (len(pieces) + 1),
        out_specs=whole,
        out_shape=jax.ShapeDtypeStruct((tokens, width), f32),
        scratch_shapes=[pltpu.VMEM((256 * len(pieces), width), bf16), pltpu.SemaphoreType.DMA((len(pieces),))],
        compiler_params=params(12),
        cost_estimate=cost(2 * tokens * 768 * width, 8 * MIB),
        name="near_part",
    )(active, base, *pieces, after)


def grad_kernel(time_ref, near_ref, act_ref, target_ref, tsum_ref, *refs):
    pieces, (out_ref, proj_ref, w_ref, sem_ref) = refs[:1], refs[1:]
    copies = [
        pltpu.make_async_copy(piece_ref, w_ref.at[k * 256 : k * 256 + 256], sem_ref.at[k])
        for k, piece_ref in enumerate(pieces)
    ]
    for copy in copies:
        copy.start()
    for copy in copies:
        copy.wait()
    width = out_ref.shape[1]
    step, group = 256, 256
    half_tokens = out_ref.shape[0] // 2
    for first in range(0, out_ref.shape[0], group):
        here_rows = slice(first, first + group)
        pp = pt = jnp.zeros((group, 128), f32)
        for n in range(width // step):
            at = slice(n * step, n * step + step)
            proj = near_ref[here_rows, at] + jnp.dot(
                act_ref[here_rows, 1792:2048], w_ref[:, at], preferred_element_type=f32
            )
            proj_ref[here_rows, at] = proj
            target = target_ref[here_rows, at]
            square, cross = proj * proj, proj * target
            pp = pp + (square[:, :128] + square[:, 128:])
            pt = pt + (cross[:, :128] + cross[:, 128:])
        for part in range(0, group, 64):
            rows = slice(first + part, first + part + 64)
            scaled = -loss_scale * (1.0 - time_ref[(first + part) // half_tokens].astype(f32) * 0.001)
            pn2 = jnp.sum(pp[part : part + 64], axis=-1, keepdims=True) + norm_eps
            cross_sum = jnp.sum(pt[part : part + 64], axis=-1, keepdims=True)
            tn2 = tsum_ref[rows, 0:1] + norm_eps
            inv = lax.rsqrt(pn2) * lax.rsqrt(tn2)
            near = scaled * inv
            along = scaled * (cross_sum * inv) / pn2
            out_ref[rows, :] = (near * target_ref[rows, :] - along * proj_ref[rows, :]).astype(bf16)


def out_grads(timesteps, near, active, target, tsum, pieces):
    tokens, width = target.shape
    whole = pl.BlockSpec(memory_space=VMEM)
    smem = pl.BlockSpec(memory_space=SMEM)
    return pl.pallas_call(
        grad_kernel,
        in_specs=[smem] + [whole] * 4 + [pl.BlockSpec(memory_space=pl.ANY)] * len(pieces),
        out_specs=whole,
        out_shape=jax.ShapeDtypeStruct((tokens, width), bf16),
        scratch_shapes=[
            pltpu.VMEM((tokens, width), f32),
            pltpu.VMEM((256, width), bf16),
            pltpu.SemaphoreType.DMA((1,)),
        ],
        compiler_params=params(20),
        cost_estimate=cost(2 * tokens * 512 * width, 15 * MIB),
        name="out_grads",
    )(timesteps, near, active, target, tsum, *pieces)


def outer_kernel(first, blocks, outs, added, *refs):
    rows_ref, grad_ref = refs[:2]
    extra_ref = refs[2] if added else None
    out_refs = refs[-len(outs) :]
    step = 256

    for n in range(grad_ref.shape[1] // step):
        at = slice(n * step, n * step + step)
        value = jnp.dot(rows_ref[first : first + blocks * 256, :], grad_ref[:, at], preferred_element_type=f32)
        if extra_ref is not None:
            value = value + extra_ref[:, at].astype(f32)
        for (start, count, dtype), out_ref in zip(outs, out_refs):
            out_ref[:, at] = value[start : start + count].astype(dtype)


def outer(rows, grad, start, count, outs, extra=None, after=None):
    tokens, width = grad.shape
    whole = pl.BlockSpec(memory_space=VMEM)
    inputs = [rows, grad] + ([] if extra is None else [extra])
    specs = [whole] * len(inputs)
    if after is not None:
        inputs, specs = inputs + [after], specs + [pl.BlockSpec(memory_space=pl.ANY)]
    return pl.pallas_call(
        functools.partial(outer_kernel, start, count // 256, outs, extra is not None),
        in_specs=specs,
        out_specs=[whole] * len(outs),
        out_shape=[jax.ShapeDtypeStruct((n, width), dtype) for _, n, dtype in outs],
        compiler_params=params(12),
        cost_estimate=cost(2 * count * tokens * width, 4 * MIB),
        name="outer",
    )(*inputs)


def whole_kernel(*refs):
    pieces, (w_ref, held_ref, sem_ref) = refs[:8], refs[-3:]
    my_y, my_x, my_c = here()
    copies, at, spots = [], 0, []
    for k, piece_ref in enumerate(pieces):
        count = piece_ref.shape[0]
        copies.append(pltpu.make_async_copy(piece_ref, held_ref.at[at : at + count], sem_ref.at[k]))
        at += count
    for copy in copies:
        copy.start()
    at = 0
    for copy, piece_ref in zip(copies, pieces):
        copy.wait()
        for _ in range(piece_ref.shape[0] // 64):
            core = (my_c + at // 1024) % 2
            row = spot_of(core, ORDER[at // 256 % 4], LINE[at // 64 % 4], my_y, my_x) * 128 + core * 64
            w_ref[pl.ds(pl.multiple_of(row, 64), 64), :] = held_ref[at : at + 64, :]
            at += 64


def whole_weight(pieces, after):
    width = pieces[0].shape[1]
    anywhere = pl.BlockSpec(memory_space=pl.ANY)
    return pl.pallas_call(
        whole_kernel,
        in_specs=[anywhere] * 9,
        out_specs=pl.BlockSpec(memory_space=VMEM),
        out_shape=jax.ShapeDtypeStruct((2048, width), bf16),
        scratch_shapes=[pltpu.VMEM((2048, width), bf16), pltpu.SemaphoreType.DMA((8,))],
        compiler_params=params(10),
        cost_estimate=cost(0, 12 * MIB),
        name="whole_weight",
    )(*pieces, after)


def pre_kernel(grad_ref, w_ref, pre_ref, *refs):
    out_ref, token_ref = refs[-2:]
    step = 256
    for k in range(pre_ref.shape[1] // step):
        at = slice(k * step, k * step + step)
        back = lax.dot_general(
            grad_ref[...], w_ref[at, :], (((1,), (1,)), ((), ())), preferred_element_type=f32
        )
        p = pre_ref[:, at].astype(f32)
        s = jax.nn.sigmoid(p)
        out_ref[:, at] = (back * (s * (1.0 + p * (1.0 - s)))).astype(bf16)
    token_ref[...] = jnp.zeros_like(token_ref)


def pre_grads(grad, weight, pre, first, count, after, old=None):
    tokens, width = grad.shape
    hidden = weight.shape[0]
    step = 512
    block = pl.BlockSpec((tokens, step), lambda i: (0, first + i))
    anywhere = pl.BlockSpec(memory_space=pl.ANY)
    inputs = [grad, weight, pre, after] + ([] if old is None else [old])
    return pl.pallas_call(
        pre_kernel,
        grid=(count,),
        in_specs=[
            pl.BlockSpec((tokens, width), lambda i: (0, 0)),
            pl.BlockSpec((step, width), lambda i: (first + i, 0)),
            block,
        ]
        + [anywhere] * (len(inputs) - 3),
        out_specs=[block, pl.BlockSpec((8, 128), lambda i: (0, 0))],
        out_shape=[jax.ShapeDtypeStruct((tokens, hidden), bf16), jax.ShapeDtypeStruct((8, 128), f32)],
        input_output_aliases={} if old is None else {4: 0},
        compiler_params=params(20, 1),
        cost_estimate=cost(2 * tokens * step * count * width, 4 * MIB * count),
        name="pre_grads",
    )(*inputs)


def summed(own, blocks, axis):
    right, left, far = blocks
    return (
        own
        + turn(right, axis, 1).astype(f32)
        + turn(left, axis, -1).astype(f32)
        + turn(far, axis, 2).astype(f32)
    )


def body(features, enc_gain, enc_bias, row_source, timesteps, pre_act, proj_weight, proj_bias):
    width = proj_weight.shape[1]
    pre = pre_act.reshape(-1, pre_act.shape[-1])
    line = [proj_weight, turn(proj_weight, FIRST, 1), turn(proj_weight, FIRST, -1), turn(proj_weight, FIRST, 2)]
    rows, active = hidden_rows(pre)
    line = pack(*line, rows)
    three, one, two = turn(line, SECOND, 1), turn(line, SECOND, -1), turn(line, SECOND, 2)
    other_line = shift(line, "c", 1)
    left, right = gate((features[:, 1:], features[:, :2]), (other_line,))
    left, right = shift(left, "z", 1), shift(right, "z", -1)
    target, tsum = make_target(row_source, left, features, right, enc_gain, enc_bias, line)
    close = near_part(active, proj_bias, [line, other_line], 0, line)
    mine = list(gate((two, one, three), (close, tsum)))
    other = [shift(piece, "c", 1) for piece in mine]
    close = near_part(active, close, mine[1:] + mine[:1], 512, line)
    close = near_part(active, close, other[1:], 1280, line)
    grad = out_grads(timesteps, close, active, target, tsum, other[:1])
    mine, other = mine + [line], other + [other_line]
    (away_far,) = outer(rows, grad, 1024, 256, ((0, 256, bf16),))
    back_far = shift(away_far, "c", 1)
    (away,) = outer(rows, grad, 1280, 768, ((0, 768, bf16),), after=away_far)
    (away,) = gate((away,), (back_far,))
    back = shift(away, "c", 1)
    (far,) = outer(rows, grad, 0, 256, ((0, 256, bf16),), back_far, after=away)
    kept_outs = ((0, 256, bf16), (256, 256, bf16), (512, 256, f32))
    to_one, to_three, own = outer(rows, grad, 256, 768, kept_outs, back, after=far)
    weight = whole_weight(mine + other, to_one)
    pre_grad, token = pre_grads(grad, weight, pre, 0, 3, to_three)
    (own,) = gate((own,), (token,))
    own = summed(own, (to_one, to_three, far), SECOND)
    blocks = {first: own[k * 64 : k * 64 + 64] for k, first in enumerate(LINE)}
    pre_grad, token = pre_grads(grad, weight, pre, 3, 1, own, pre_grad)
    (kept,) = gate((blocks[0],), (token,))
    block = summed(kept, [blocks[d].astype(bf16) for d in (1, 3, 2)], FIRST).astype(bf16)
    parts = lax.all_to_all(block, "z", 0, 0, tiled=True)
    total = jnp.sum(parts.reshape(8, 8, width).astype(f32), axis=0).astype(bf16)
    total = jnp.broadcast_to(total[None], (8, 8, width)).reshape(block.shape)
    weight_grad = lax.all_to_all(total, "z", 0, 0, tiled=True).astype(f32)
    return (pre_grad.reshape(pre_act.shape), weight_grad)


def solution(mesh):
    fine = Mesh(mesh.devices.reshape(4, 4, 2, 8), ("y", "x", "c", "z"))
    dp = ("y", "x", "c")
    return jax.shard_map(
        body,
        mesh=fine,
        in_specs=(
            P(dp, "z", None, None),
            P(),
            P(),
            P(dp, "z"),
            P(dp),
            P(dp, "z", None, None),
            P(dp, None),
            P(),
        ),
        out_specs=(P(dp, "z", None, None), P(dp, None)),
        check_vma=False,
    )
```

```python
import functools

import jax
import jax.numpy as jnp
from jax import lax
from jax.experimental import pallas as pl
from jax.experimental.pallas import tpu as pltpu
from jax.sharding import Mesh, PartitionSpec as P

loss_scale = 1024.0
norm_eps = 1e-06
MIB = 1 << 20
bf16, f32 = jnp.bfloat16, jnp.float32
VMEM = pltpu.VMEM
SMEM = pltpu.SMEM


def shift(block, axis, step):
    count = lax.axis_size(axis)
    return lax.ppermute(block, axis, [(i, (i + step) % count) for i in range(count)])


def turn(block, order, step):
    pairs = []
    for y in range(4):
        for x in range(4):
            for c in range(2):
                along_x = (c == 0) == (order == 0)
                to_y, to_x = (y, (x + step) % 4) if along_x else ((y + step) % 4, x)
                pairs.append(((y * 4 + x) * 2 + c, (to_y * 4 + to_x) * 2 + c))
    return lax.ppermute(block, ("y", "x", "c"), pairs)


FIRST, SECOND = 0, 1
LINE = (0, 3, 1, 2)
ORDER = (2, 1, 3, 0)


def params(mib, steps=0):
    semantics = ("arbitrary",) * steps if steps else None
    return pltpu.CompilerParams(vmem_limit_bytes=mib * MIB, dimension_semantics=semantics)


def cost(flops, nbytes, trans=0):
    return pl.CostEstimate(flops=flops // 64, bytes_accessed=nbytes // 64, transcendentals=trans // 64)


def gate_kernel(*refs):
    pass


def gate(arrays, after):
    anywhere = pl.BlockSpec(memory_space=pl.ANY)
    return pl.pallas_call(
        gate_kernel,
        in_specs=[anywhere] * (len(arrays) + len(after)),
        out_specs=[anywhere] * len(arrays),
        out_shape=[jax.ShapeDtypeStruct(array.shape, array.dtype) for array in arrays],
        input_output_aliases={k: k for k in range(len(arrays))},
        compiler_params=params(1),
        cost_estimate=cost(0, 0),
        name="gate",
    )(*arrays, *after)


def pack_kernel(own_ref, left_ref, right_ref, far_ref, after_ref, out_ref):
    for k, ref in enumerate((own_ref, left_ref, right_ref, far_ref)):
        out_ref[k * 64 : k * 64 + 64, :] = ref[...]


def pack(own, left, right, far, after):
    whole = pl.BlockSpec(memory_space=VMEM)
    return pl.pallas_call(
        pack_kernel,
        in_specs=[whole] * 4 + [pl.BlockSpec(memory_space=pl.ANY)],
        out_specs=whole,
        out_shape=jax.ShapeDtypeStruct((256, own.shape[1]), bf16),
        compiler_params=params(4),
        cost_estimate=cost(0, MIB),
        name="pack",
    )(own, left, right, far, after)


def spot_of(core, second, first, my_y, my_x):
    y = jnp.where(core == 0, my_y + second, my_y + first) % 4
    x = jnp.where(core == 0, my_x + first, my_x + second) % 4
    return y * 4 + x


def here():
    return lax.axis_index("y"), lax.axis_index("x"), lax.axis_index("c")


def silu_kernel(pre_ref, rows_ref, act_ref):
    step = pl.program_id(0)
    my_y, my_x, my_c = here()
    dy = (step // 4 - my_y + 4) % 4
    dx = (step % 4 - my_x + 4) % 4
    p = pre_ref[...].astype(f32)
    active = (p * jax.nn.sigmoid(p)).astype(bf16)
    turned = active.T
    for c in range(2):
        dc = (c - my_c + 2) % 2
        second, first = (dy, dx) if c == 0 else (dx, dy)
        block = jnp.where(second == 2, 0, jnp.where(second == 0, 3, jnp.where(second == 1, 1, 2)))
        spot = jnp.where(first == 0, 0, jnp.where(first == 3, 1, first + 1))
        row = pl.multiple_of(dc * 1024 + block * 256 + spot * 64, 64)
        rows_ref[pl.ds(row, 64), :] = turned[c * 64 : c * 64 + 64, :]

    @pl.when(step == pl.num_programs(0) - 1)
    def _():
        for at, k in enumerate((6, 7, 14, 15, 2, 3, 4, 5, 0, 1, 10, 11, 12, 13, 8, 9)):
            act_ref[:, at * 128 : at * 128 + 128] = rows_ref[k * 128 : k * 128 + 128, :].T


def hidden_rows(pre):
    tokens, hidden = pre.shape
    return pl.pallas_call(
        silu_kernel,
        grid=(hidden // 128,),
        in_specs=[pl.BlockSpec((tokens, 128), lambda i: (0, i))],
        out_specs=[
            pl.BlockSpec((hidden, tokens), lambda i: (0, 0)),
            pl.BlockSpec((tokens, hidden), lambda i: (0, 0)),
        ],
        out_shape=[jax.ShapeDtypeStruct((hidden, tokens), bf16), jax.ShapeDtypeStruct((tokens, hidden), bf16)],
        compiler_params=params(20, 1),
        cost_estimate=cost(tokens * hidden * 8, tokens * hidden * 6, tokens * hidden),
        name="hidden_rows",
    )(pre)


def target_kernel(source_ref, left_ref, mid_ref, right_ref, gain_ref, bias_ref, after_ref, out_ref, sum_ref, ext_ref):
    gain, bias = gain_ref[...].reshape(1, -1), bias_ref[...].reshape(1, -1)
    width = gain.shape[-1]
    offset = lax.axis_index("z") * 3 - 2
    for b in range(2):
        row = 0
        for ref, count in ((left_ref, 2), (mid_ref, 3), (right_ref, 2)):
            for k in range(count):
                x = ref[b, k].astype(f32)
                center = x - jnp.sum(x, axis=-1, keepdims=True) * (1.0 / width)
                spread = jnp.sum(center * center, axis=-1, keepdims=True) * (1.0 / width)
                ext_ref[b, row : row + 32, :] = (center * lax.rsqrt(spread + norm_eps) * gain + bias).astype(bf16)
                row += 32
    c = lax.broadcasted_iota(jnp.int32, (64, 224), 0)
    lane = lax.broadcasted_iota(jnp.int32, (64, 224), 1)
    source, j = lane // 32, lane % 32
    odd = c % 2 == 1
    low = jnp.where(odd, (c - 1) // 2, c // 2 - 1)
    high_w = jnp.where(odd, 0.25, 0.75).astype(f32)
    columns = jnp.where(j == jnp.clip(low, 0, 31), 1.0 - high_w, 0.0) + jnp.where(
        j == jnp.clip(low + 1, 0, 31), high_w, 0.0
    )
    for b in range(2):
        for r in range(6):
            h = 0.25 if r % 2 == 1 else 0.75
            first = source_ref[b, r] - offset
            rows = jnp.where(source == first, 1.0 - h, 0.0) + jnp.where(source == first + 1, h, 0.0)
            blend = (columns * rows).astype(bf16)
            target = jnp.dot(blend, ext_ref[b], preferred_element_type=f32)
            at = (b * 6 + r) * 64
            out_ref[at : at + 64, :] = target
            sum_ref[at : at + 64, :] = jnp.broadcast_to(jnp.sum(target * target, axis=-1, keepdims=True), (64, 128))


def make_target(row_source, left, mid, right, gain, bias, after):
    width = gain.shape[-1]
    whole = pl.BlockSpec(memory_space=VMEM)
    return pl.pallas_call(
        target_kernel,
        in_specs=[pl.BlockSpec(memory_space=SMEM)] + [whole] * 5 + [pl.BlockSpec(memory_space=pl.ANY)],
        out_specs=[whole, whole],
        out_shape=[jax.ShapeDtypeStruct((768, width), f32), jax.ShapeDtypeStruct((768, 128), f32)],
        scratch_shapes=[pltpu.VMEM((2, 224, width), bf16)],
        compiler_params=params(16),
        cost_estimate=cost(2 * 768 * 224 * width, 768 * width * 8),
        name="make_target",
    )(row_source, left, mid, right, gain, bias, after)


def near_kernel(first, has_base, act_ref, base_ref, *refs):
    pieces, (out_ref, w_ref, sem_ref) = refs[:-4], refs[-3:]
    copies = [
        pltpu.make_async_copy(piece_ref, w_ref.at[k * 256 : k * 256 + 256], sem_ref.at[k])
        for k, piece_ref in enumerate(pieces)
    ]
    for copy in copies:
        copy.start()
    for copy in copies:
        copy.wait()
    step = 256
    for n in range(out_ref.shape[1] // step):
        at = slice(n * step, n * step + step)
        base = base_ref[:, at] if has_base else base_ref[at].reshape(1, -1)
        out_ref[:, at] = base + jnp.dot(act_ref[:, first : first + w_ref.shape[0]], w_ref[:, at], preferred_element_type=f32)


def near_part(active, base, pieces, first, after):
    tokens = active.shape[0]
    width = base.shape[-1]
    whole = pl.BlockSpec(memory_space=VMEM)
    anywhere = pl.BlockSpec(memory_space=pl.ANY)
    return pl.pallas_call(
        functools.partial(near_kernel, first, base.ndim == 2),
        in_specs=[whole] * 2 + [anywhere] * (len(pieces) + 1),
        out_specs=whole,
        out_shape=jax.ShapeDtypeStruct((tokens, width), f32),
        scratch_shapes=[pltpu.VMEM((256 * len(pieces), width), bf16), pltpu.SemaphoreType.DMA((len(pieces),))],
        compiler_params=params(12),
        cost_estimate=cost(2 * tokens * 768 * width, 8 * MIB),
        name="near_part",
    )(active, base, *pieces, after)


def grad_kernel(time_ref, near_ref, act_ref, target_ref, tsum_ref, *refs):
    pieces, (rows_ref, out_ref, away_ref, own_ref, proj_ref, sum_ref, w_ref, sem_ref) = refs[:1], refs[1:]
    copies = [
        pltpu.make_async_copy(piece_ref, w_ref.at[k * 256 : k * 256 + 256], sem_ref.at[k])
        for k, piece_ref in enumerate(pieces)
    ]
    for copy in copies:
        copy.start()
    for copy in copies:
        copy.wait()
    width = out_ref.shape[1]
    step, group = 256, 256
    half_tokens = out_ref.shape[0] // 2
    for first in range(0, out_ref.shape[0], group):
        here_rows = slice(first, first + group)
        pp = pt = jnp.zeros((group, 128), f32)
        for n in range(width // step):
            at = slice(n * step, n * step + step)
            proj = near_ref[here_rows, at] + jnp.dot(
                act_ref[here_rows, 1792:2048], w_ref[:, at], preferred_element_type=f32
            )
            proj_ref[here_rows, at] = proj
            target = target_ref[here_rows, at]
            square, cross = proj * proj, proj * target
            pp = pp + (square[:, :128] + square[:, 128:])
            pt = pt + (cross[:, :128] + cross[:, 128:])
        for part in range(0, group, 64):
            rows = slice(first + part, first + part + 64)
            scaled = -loss_scale * (1.0 - time_ref[(first + part) // half_tokens].astype(f32) * 0.001)
            pn2 = jnp.sum(pp[part : part + 64], axis=-1, keepdims=True) + norm_eps
            cross_sum = jnp.sum(pt[part : part + 64], axis=-1, keepdims=True)
            tn2 = tsum_ref[rows, 0:1] + norm_eps
            inv = lax.rsqrt(pn2) * lax.rsqrt(tn2)
            near = scaled * inv
            along = scaled * (cross_sum * inv) / pn2
            out_ref[rows, :] = (near * target_ref[rows, :] - along * proj_ref[rows, :]).astype(bf16)
        far_rows = jnp.concatenate([rows_ref[1024:1280, here_rows], rows_ref[0:256, here_rows]], axis=0)
        term = jnp.dot(far_rows, out_ref[here_rows, :], preferred_element_type=f32)
        sum_ref[...] = term if first == 0 else sum_ref[...] + term
    away_ref[...] = sum_ref[0:256, :].astype(bf16)
    own_ref[...] = sum_ref[256:512, :]


def out_grads(timesteps, near, active, target, tsum, pieces, rows):
    tokens, width = target.shape
    whole = pl.BlockSpec(memory_space=VMEM)
    smem = pl.BlockSpec(memory_space=SMEM)
    return pl.pallas_call(
        grad_kernel,
        in_specs=[smem] + [whole] * 4 + [pl.BlockSpec(memory_space=pl.ANY)] * len(pieces) + [whole],
        out_specs=[whole] * 3,
        out_shape=[
            jax.ShapeDtypeStruct((tokens, width), bf16),
            jax.ShapeDtypeStruct((256, width), bf16),
            jax.ShapeDtypeStruct((256, width), f32),
        ],
        scratch_shapes=[
            pltpu.VMEM((tokens, width), f32),
            pltpu.VMEM((512, width), f32),
            pltpu.VMEM((256, width), bf16),
            pltpu.SemaphoreType.DMA((1,)),
        ],
        compiler_params=params(24),
        cost_estimate=cost(2 * tokens * 512 * width, 15 * MIB),
        name="out_grads",
    )(timesteps, near, active, target, tsum, *pieces, rows)


def outer_kernel(first, blocks, outs, added, *refs):
    rows_ref, grad_ref = refs[:2]
    extra_ref = refs[2] if added else None
    out_refs = refs[-len(outs) :]
    step = 256

    for n in range(grad_ref.shape[1] // step):
        at = slice(n * step, n * step + step)
        value = jnp.dot(rows_ref[first : first + blocks * 256, :], grad_ref[:, at], preferred_element_type=f32)
        if extra_ref is not None:
            value = value + extra_ref[:, at].astype(f32)
        for (start, count, dtype), out_ref in zip(outs, out_refs):
            out_ref[:, at] = value[start : start + count].astype(dtype)


def outer(rows, grad, start, count, outs, extra=None, after=None):
    tokens, width = grad.shape
    whole = pl.BlockSpec(memory_space=VMEM)
    inputs = [rows, grad] + ([] if extra is None else [extra])
    specs = [whole] * len(inputs)
    if after is not None:
        inputs, specs = inputs + [after], specs + [pl.BlockSpec(memory_space=pl.ANY)]
    return pl.pallas_call(
        functools.partial(outer_kernel, start, count // 256, outs, extra is not None),
        in_specs=specs,
        out_specs=[whole] * len(outs),
        out_shape=[jax.ShapeDtypeStruct((n, width), dtype) for _, n, dtype in outs],
        compiler_params=params(12),
        cost_estimate=cost(2 * count * tokens * width, 4 * MIB),
        name="outer",
    )(*inputs)


def whole_kernel(*refs):
    pieces, (w_ref, held_ref, sem_ref) = refs[:8], refs[-3:]
    my_y, my_x, my_c = here()
    copies, at, spots = [], 0, []
    for k, piece_ref in enumerate(pieces):
        count = piece_ref.shape[0]
        copies.append(pltpu.make_async_copy(piece_ref, held_ref.at[at : at + count], sem_ref.at[k]))
        at += count
    for copy in copies:
        copy.start()
    at = 0
    for copy, piece_ref in zip(copies, pieces):
        copy.wait()
        for _ in range(piece_ref.shape[0] // 64):
            core = (my_c + at // 1024) % 2
            row = spot_of(core, ORDER[at // 256 % 4], LINE[at // 64 % 4], my_y, my_x) * 128 + core * 64
            w_ref[pl.ds(pl.multiple_of(row, 64), 64), :] = held_ref[at : at + 64, :]
            at += 64


def whole_weight(pieces, after):
    width = pieces[0].shape[1]
    anywhere = pl.BlockSpec(memory_space=pl.ANY)
    return pl.pallas_call(
        whole_kernel,
        in_specs=[anywhere] * 9,
        out_specs=pl.BlockSpec(memory_space=VMEM),
        out_shape=jax.ShapeDtypeStruct((2048, width), bf16),
        scratch_shapes=[pltpu.VMEM((2048, width), bf16), pltpu.SemaphoreType.DMA((8,))],
        compiler_params=params(10),
        cost_estimate=cost(0, 12 * MIB),
        name="whole_weight",
    )(*pieces, after)


def pre_kernel(grad_ref, w_ref, pre_ref, *refs):
    out_ref, token_ref = refs[-2:]
    step = 256
    for k in range(pre_ref.shape[1] // step):
        at = slice(k * step, k * step + step)
        back = lax.dot_general(
            grad_ref[...], w_ref[at, :], (((1,), (1,)), ((), ())), preferred_element_type=f32
        )
        p = pre_ref[:, at].astype(f32)
        s = jax.nn.sigmoid(p)
        out_ref[:, at] = (back * (s * (1.0 + p * (1.0 - s)))).astype(bf16)
    token_ref[...] = jnp.zeros_like(token_ref)


def pre_grads(grad, weight, pre, first, count, after, old=None):
    tokens, width = grad.shape
    hidden = weight.shape[0]
    step = 512
    block = pl.BlockSpec((tokens, step), lambda i: (0, first + i))
    anywhere = pl.BlockSpec(memory_space=pl.ANY)
    inputs = [grad, weight, pre, after] + ([] if old is None else [old])
    return pl.pallas_call(
        pre_kernel,
        grid=(count,),
        in_specs=[
            pl.BlockSpec((tokens, width), lambda i: (0, 0)),
            pl.BlockSpec((step, width), lambda i: (first + i, 0)),
            block,
        ]
        + [anywhere] * (len(inputs) - 3),
        out_specs=[block, pl.BlockSpec((8, 128), lambda i: (0, 0))],
        out_shape=[jax.ShapeDtypeStruct((tokens, hidden), bf16), jax.ShapeDtypeStruct((8, 128), f32)],
        input_output_aliases={} if old is None else {4: 0},
        compiler_params=params(20, 1),
        cost_estimate=cost(2 * tokens * step * count * width, 4 * MIB * count),
        name="pre_grads",
    )(*inputs)


def summed(own, blocks, axis):
    right, left, far = blocks
    return (
        own
        + turn(right, axis, 1).astype(f32)
        + turn(left, axis, -1).astype(f32)
        + turn(far, axis, 2).astype(f32)
    )


def body(features, enc_gain, enc_bias, row_source, timesteps, pre_act, proj_weight, proj_bias):
    width = proj_weight.shape[1]
    pre = pre_act.reshape(-1, pre_act.shape[-1])
    line = [proj_weight, turn(proj_weight, FIRST, 1), turn(proj_weight, FIRST, -1), turn(proj_weight, FIRST, 2)]
    rows, active = hidden_rows(pre)
    line = pack(*line, rows)
    three, one, two = turn(line, SECOND, 1), turn(line, SECOND, -1), turn(line, SECOND, 2)
    other_line = shift(line, "c", 1)
    left, right = gate((features[:, 1:], features[:, :2]), (other_line,))
    left, right = shift(left, "z", 1), shift(right, "z", -1)
    target, tsum = make_target(row_source, left, features, right, enc_gain, enc_bias, line)
    close = near_part(active, proj_bias, [line, other_line], 0, line)
    mine = list(gate((two, one, three), (close, tsum)))
    other = [shift(piece, "c", 1) for piece in mine]
    close = near_part(active, close, mine[1:] + mine[:1], 512, line)
    close = near_part(active, close, other[1:], 1280, line)
    grad, away_far, far = out_grads(timesteps, close, active, target, tsum, other[:1], rows)
    mine, other = mine + [line], other + [other_line]
    back_far = shift(away_far, "c", 1)
    (away,) = outer(rows, grad, 1280, 768, ((0, 768, bf16),), after=away_far)
    (away,) = gate((away,), (back_far,))
    back = shift(away, "c", 1)
    far = (far + back_far.astype(f32)).astype(bf16)
    kept_outs = ((0, 256, bf16), (256, 256, bf16), (512, 256, f32))
    to_one, to_three, own = outer(rows, grad, 256, 768, kept_outs, back, after=far)
    weight = whole_weight(mine + other, to_one)
    pre_grad, token = pre_grads(grad, weight, pre, 0, 3, to_three)
    (own,) = gate((own,), (token,))
    own = summed(own, (to_one, to_three, far), SECOND)
    blocks = {first: own[k * 64 : k * 64 + 64] for k, first in enumerate(LINE)}
    pre_grad, token = pre_grads(grad, weight, pre, 3, 1, own, pre_grad)
    (kept,) = gate((blocks[0],), (token,))
    block = summed(kept, [blocks[d].astype(bf16) for d in (1, 3, 2)], FIRST).astype(bf16)
    parts = lax.all_to_all(block, "z", 0, 0, tiled=True)
    total = jnp.sum(parts.reshape(8, 8, width).astype(f32), axis=0).astype(bf16)
    total = jnp.broadcast_to(total[None], (8, 8, width)).reshape(block.shape)
    weight_grad = lax.all_to_all(total, "z", 0, 0, tiled=True).astype(f32)
    return (pre_grad.reshape(pre_act.shape), weight_grad)


def solution(mesh):
    fine = Mesh(mesh.devices.reshape(4, 4, 2, 8), ("y", "x", "c", "z"))
    dp = ("y", "x", "c")
    return jax.shard_map(
        body,
        mesh=fine,
        in_specs=(
            P(dp, "z", None, None),
            P(),
            P(),
            P(dp, "z"),
            P(dp),
            P(dp, "z", None, None),
            P(dp, None),
            P(),
        ),
        out_specs=(P(dp, "z", None, None), P(dp, None)),
        check_vma=False,
    )
```
